512 devices in a mesh: dp: 32 (over z_lo, y, core), tensor: 16 (over z_hi, x).
Axes of the slice: x: 4, y: 8, z: 8 (z_hi: 4, z_lo: 2; z = z_hi * 2 + z_lo), core: 2. Of those that a mesh axis runs over, the one named last changes fastest.
Arguments:
- inputs: bfloat16 [32, 128, 5120], P('dp', None, 'tensor'), may hold values from -6 to 6
- w_qkv: bfloat16 [3, 5120, 4096], P(None, 'dp', 'tensor'), may hold values from -0.078125 to 0.078125
- w_gates: bfloat16 [2, 5120, 32], P(None, None, 'tensor'), may hold values from -0.078125 to 0.078125
- conv_weight: float32 [3, 4, 4096], P(None, None, 'tensor'), may hold values from -3 to 3
- decay_rate: float32 [32], P('tensor'), may hold values from 0.002 to 0.1
- gate_bias: float32 [32], P('tensor'), may hold values from -2 to 2
- norm_gain: float32 [128], replicated, may hold values from 0.5 to 1.5
- w_out: bfloat16 [4096, 5120], P('tensor', 'dp'), may hold values from -0.09375 to 0.09375
- grad_out: bfloat16 [32, 128, 5120], P('dp', None, 'tensor'), may hold values from -0.1796875 to 0.1796875
Outputs:
- output: bfloat16 [32, 128, 5120], P('dp', None, 'tensor')
- grad_in: bfloat16 [32, 128, 5120], P('dp', None, 'tensor')
- grad_gates: float32 [2, 5120, 32], P(None, None, 'tensor')
- grad_conv: float32 [3, 4, 4096], P(None, None, 'tensor')
- grad_rate: float32 [32], P('tensor')
- grad_bias: float32 [32], P('tensor')
- grad_gain: float32 [128], replicated
The draws below stay inside these ranges and needn't reach their ends.
All inputs are finite; a program needn't handle non-finite values.
Results may differ from the reference program's by a relative error of at most 0.019.
Values may be sent and summed in bfloat16 or wider, within the bound.
A program may use at most 64 MiB of HBM per device.

```python
import math
import jax
import jax.numpy as jnp
from jax import lax

D = 5120
HEADS = 32
DK = 128
DV = 128
KERNEL = 4
BLOCK = 64
LEN = 128
BATCH = 32
N_TENSOR = 16


def levels(stream_key, shape, shards, least, high):
    def one(dim, blocks):
        steps = jax.random.uniform(jax.random.fold_in(jax.random.fold_in(stream_key, 6), dim), (blocks,), jnp.float32, least / len(shards), high / len(shards))
        return jnp.repeat(jnp.exp(steps), shape[dim] // blocks).reshape((-1,) + (1,) * (len(shape) - dim - 1))

    factor_of = one(*shards[0])
    for cut in shards[1:]:
        factor_of = factor_of * one(*cut)
    return factor_of


def normal_values(rng, dims, width, limit, cuts=(), kind=jnp.bfloat16):
    loudness = levels(rng, dims, cuts, -0.22, 0.18) if cuts else 1.0
    values = jax.random.normal(rng, dims, jnp.float32) * width * loudness
    return jnp.minimum(jnp.maximum(values, -limit), limit).astype(kind)


def setup_inputs(seed: int = 0) -> dict:
    seeds = jax.random.split(jax.random.key(seed), 10)
    return {
        "inputs": normal_values(seeds[0], (BATCH, LEN, D), 1.0, 6.0, ((0, 32), (2, 16))),
        "w_qkv": normal_values(seeds[1], (3, D, HEADS * DK), D ** -0.5, 0.078125, ((1, 32), (2, 16))),
        "w_gates": normal_values(seeds[2], (2, D, HEADS), D ** -0.5, 0.078125, ((2, 16),)),
        "conv_weight": normal_values(seeds[3], (3, KERNEL, HEADS * DK), KERNEL ** -0.5, 3.0, ((2, 16),), jnp.float32),
        "decay_rate": jnp.clip(jnp.exp(math.log(0.1) - 3.912023 * jax.random.uniform(seeds[4], (HEADS,), jnp.float32) ** levels(seeds[4], (HEADS,), ((0, 16),), -0.2, 0.2)), 0.002, 0.1),
        "gate_bias": jnp.clip(jax.random.uniform(seeds[5], (HEADS,), jnp.float32, -2.0, 2.0) * levels(seeds[5], (HEADS,), ((0, 16),), -0.4, 0.0), -2.0, 2.0),
        "norm_gain": jnp.clip(1.0 + 0.1 * jax.random.normal(seeds[6], (DV,), jnp.float32), 0.5, 1.5),
        "w_out": normal_values(seeds[7], (HEADS * DV, D), (HEADS * DV) ** -0.5, 0.09375, ((0, 16), (1, 32))),
        "grad_out": normal_values(seeds[8], (BATCH, LEN, D), 0.03, 0.1796875, ((0, 32), (2, 16))),
    }


HI = lax.Precision.HIGHEST

def head_scan(queries, key_rows, value_rows, decays, strength):
    block_count = queries.shape[0] // BLOCK

    def to_blocks(array):
        return array.reshape((block_count, BLOCK) + array.shape[1:])
    position = jnp.arange(BLOCK)
    strict = position[:, None] > position[None, :]
    within = position[:, None] >= position[None, :]

    def advance(carried, block_items):
        query_part, key_part, value_part, decay_part, write_part = block_items
        cumulative = jnp.cumsum(decay_part)
        spread = jnp.where(within, cumulative[:, None] - cumulative[None, :], 0.0)
        fading = jnp.where(within, jnp.exp(spread), 0.0)
        key_dots = jnp.dot(key_part, key_part.T, precision=HI)
        system = jnp.eye(BLOCK, dtype=queries.dtype) + write_part[:, None] * jnp.where(strict, fading * key_dots, 0.0)
        growth = jnp.exp(cumulative)[:, None]
        target = write_part[:, None] * (value_part - growth * jnp.dot(key_part, carried.T, precision=HI))
        update_rows = jax.scipy.linalg.solve_triangular(system, target, lower=True, unit_diagonal=True)
        scores = fading * jnp.dot(query_part, key_part.T, precision=HI)
        result = growth * jnp.dot(query_part, carried.T, precision=HI) + jnp.dot(scores, update_rows, precision=HI)
        remain = jnp.exp(cumulative[-1] - cumulative)[:, None]
        carried = jnp.exp(cumulative[-1]) * carried + jnp.dot((update_rows * remain).T, key_part, precision=HI)
        return (carried, result)
    initial = jnp.zeros((value_rows.shape[1], key_rows.shape[1]), queries.dtype)
    _, results = lax.scan(advance, initial, (to_blocks(queries), to_blocks(key_rows), to_blocks(value_rows), to_blocks(decays), to_blocks(strength)))
    return results.reshape(queries.shape[0], value_rows.shape[1])

def layer_core(projected, logits, conv_weight, decay_rate, gate_bias, norm_gain):
    length = projected.shape[1]
    head_count = decay_rate.shape[0]
    tap_count = conv_weight.shape[1]
    padded = jnp.pad(projected, ((0, 0), (tap_count - 1, 0), (0, 0)))
    convolved = conv_weight[:, 0][:, None, :] * padded[:, 0:length]
    for offset in range(1, tap_count):
        convolved = convolved + conv_weight[:, offset][:, None, :] * padded[:, offset:offset + length]
    active = jax.nn.silu(convolved).reshape(3, length, head_count, -1)
    head_width = active.shape[-1]
    queries = active[0] / jnp.sqrt(lax.optimization_barrier(jnp.sum(active[0] * active[0], -1, keepdims=True)) + 1e-06) / math.sqrt(head_width)
    key_rows = active[1] / jnp.sqrt(lax.optimization_barrier(jnp.sum(active[1] * active[1], -1, keepdims=True)) + 1e-06)
    value_rows = active[2]
    strength = jax.nn.sigmoid(logits[1])
    decays = -decay_rate * jax.nn.softplus(logits[0] + gate_bias)
    heads_out = jax.vmap(head_scan, in_axes=(1, 1, 1, 1, 1), out_axes=1)(queries, key_rows, value_rows, decays, strength)
    row_scale = jnp.sqrt(lax.optimization_barrier(jnp.mean(heads_out * heads_out, -1, keepdims=True)) + 1e-05)
    normed = heads_out / row_scale * norm_gain
    return normed.reshape(length, -1)

def rounded(values):
    return lax.optimization_barrier(values.astype(jnp.bfloat16)).astype(jnp.float32)

def reference(inputs, w_qkv, w_gates, conv_weight, decay_rate, gate_bias, norm_gain, w_out, grad_out):
    groups = N_TENSOR
    qkv_wide = w_qkv.astype(jnp.float32)
    gate_wide = w_gates.astype(jnp.float32)
    out_wide = w_out.astype(jnp.float32)
    group_cols = qkv_wide.reshape(3, D, groups, -1)
    gate_cols = gate_wide.reshape(2, D, groups, -1)
    out_rows = out_wide.reshape(groups, -1, D)

    def per_sequence(pair):
        sequence = pair[0].astype(jnp.float32)
        cotangent = pair[1].astype(jnp.float32)
        projected = jnp.einsum('ld,sdc->slc', sequence, qkv_wide)
        logits = jnp.einsum('ld,sdh->slh', sequence, gate_wide)
        core_out, pullback = jax.vjp(layer_core, projected, logits, conv_weight, decay_rate, gate_bias, norm_gain)
        core_low = rounded(core_out)
        group_parts = jnp.einsum('lgc,gcd->lgd', core_low.reshape(LEN, groups, -1), out_rows)
        output = lax.optimization_barrier(jnp.sum(rounded(group_parts), axis=1)).astype(jnp.bfloat16)
        core_grad = jnp.einsum('ld,cd->lc', cotangent, out_wide)
        proj_grad, logit_grad, conv_grad, rate_grad, bias_grad, gain_grad = pullback(core_grad)
        proj_low = rounded(proj_grad)
        logit_low = rounded(logit_grad)
        back_parts = jnp.einsum('slgc,sdgc->lgd', proj_low.reshape(3, LEN, groups, -1), group_cols)
        back_parts = back_parts + jnp.einsum('slgh,sdgh->lgd', logit_low.reshape(2, LEN, groups, -1), gate_cols)
        grad_in = lax.optimization_barrier(jnp.sum(rounded(back_parts), axis=1)).astype(jnp.bfloat16)
        gate_grad = jnp.einsum('ld,slh->sdh', sequence, logit_low)
        return (output, grad_in, gate_grad, conv_grad, rate_grad, bias_grad, gain_grad)
    results = lax.map(per_sequence, (inputs, grad_out))
    return (results[0], results[1], lax.optimization_barrier(jnp.sum(results[2], 0)), lax.optimization_barrier(jnp.sum(results[3], 0)), lax.optimization_barrier(jnp.sum(results[4], 0)), lax.optimization_barrier(jnp.sum(results[5], 0)), lax.optimization_barrier(jnp.sum(results[6], 0)))
```

```python
import functools
import math

import jax
import jax.numpy as jnp
from jax import lax
from jax.experimental import pallas as pl
from jax.experimental.pallas import tpu as pltpu
from jax.sharding import PartitionSpec as P

MESH = pl.DeviceIdType.MESH
F32, BF16 = jnp.float32, jnp.bfloat16
LEN = 128
HEAD = 128
TAPS = 4
CORES = 2
ZL = 2
NN = (((1,), (0,)), ((), ()))
NT = (((1,), (1,)), ((), ()))


class Place:
    def __init__(self, dp, tensor):
        self.ny = dp // (ZL * CORES)
        self.nz = 4 if tensor == 16 else 2
        self.nx = tensor // self.nz
        d, t = lax.axis_index("dp"), lax.axis_index("tensor")
        self.d, self.t = d, t
        self.zl = d // (self.ny * CORES)
        self.y = (d // CORES) % self.ny
        self.c = d % CORES
        self.zh = t // self.nx
        self.x = t % self.nx

    def dp_of(self, zl, y, c):
        return zl * (self.ny * CORES) + y * CORES + c

    def at_y(self, step):
        return self.dp_of(self.zl, (self.y + step + self.ny) % self.ny, self.c), self.t

    def at_z(self):
        return self.dp_of(1 - self.zl, self.y, self.c), self.t

    def at_core(self):
        return self.dp_of(self.zl, self.y, 1 - self.c), self.t

    def at_zh(self, step):
        return self.d, ((self.zh + step + self.nz) % self.nz) * self.nx + self.x

    def at_x(self, step):
        return self.d, self.zh * self.nx + (self.x + step + self.nx) % self.nx


def remote(src, dst, send, recv, where):
    return pltpu.make_async_remote_copy(
        src_ref=src, dst_ref=dst, send_sem=send, recv_sem=recv, device_id=where, device_id_type=MESH
    )


def meet(peers):
    barrier = pltpu.get_barrier_semaphore()
    for where in peers:
        pl.semaphore_signal(barrier, inc=1, device_id=where, device_id_type=MESH)
    pl.semaphore_wait(barrier, len(peers))


def gather_kernel(
    dp, tensor, w_ref, x_ref, g_ref, wf_ref, xf_ref, gf_ref, own_sem,
    yp_s, yp_r, ym_s, ym_r, z_s, z_r, c_s, c_r, t1_s, t1_r, t2_s, t2_r,
):
    here = Place(dp, tensor)
    ny, nz, nx = here.ny, here.nz, here.nx
    far = ny // 2
    shard = w_ref.shape[1]
    half = shard // 2
    meet(
        [here.at_y(1), here.at_y(-1), here.at_z(), here.at_core()]
        + [here.at_zh(s) for s in range(1, nz)]
        + [here.at_x(s) for s in range(1, nx)]
    )

    def block(zl, y, c, h):
        row = pl.multiple_of(here.dp_of(zl, y, c) * shard + h * half, 16)
        return wf_ref.at[:, pl.ds(row, half), :]

    own = [
        pltpu.make_async_copy(w_ref, wf_ref.at[:, pl.ds(pl.multiple_of(here.d * shard, 16), shard), :], own_sem.at[0]),
        pltpu.make_async_copy(x_ref, xf_ref.at[here.t], own_sem.at[1]),
        pltpu.make_async_copy(g_ref, gf_ref.at[here.t], own_sem.at[2]),
    ]
    for copy in own:
        copy.start()
    sent = []

    def send(src, dst, s, r, where):
        copy = remote(src, dst, s, r, where)
        copy.start()
        sent.append(copy)

    def arrive(dst, s, r):
        remote(dst, dst, s, r, here.at_core()).wait_recv()

    def travels(direction, k, h):
        return k < far or (k == far and h == (0 if direction > 0 else 1))

    def y_sems(direction):
        return (yp_s, yp_r) if direction > 0 else (ym_s, ym_r)

    def on_y(src, dst, direction, k, p, h):
        if k <= far and travels(direction, k, h):
            s, r = y_sems(direction)
            send(src, dst, s.at[k - 1, p, h], r.at[k - 1, p, h], here.at_y(direction))

    mine = [w_ref.at[:, pl.ds(h * half, half), :] for h in range(2)]
    for h in range(2):
        dst = block(here.zl, here.y, here.c, h)
        send(mine[h], dst, z_s.at[h], z_r.at[h], here.at_z())
        on_y(mine[h], dst, 1, 1, 0, h)
        on_y(mine[h], dst, -1, 1, 0, h)
    arrays = ((x_ref, xf_ref), (g_ref, gf_ref))
    for a, (src, dst) in enumerate(arrays):
        for s in range(1, nz):
            send(src, dst.at[here.t], t1_s.at[s - 1, a], t1_r.at[s - 1, a], here.at_zh(s))
    for a, (src, dst) in enumerate(arrays):
        for s in range(1, nx):
            send(src, dst.at[here.t], t2_s.at[s - 1, 0, a], t2_r.at[s - 1, 0, a], here.at_x(s))
    for h in range(2):
        dst = block(here.zl, here.y, here.c, h)
        send(mine[h], dst, c_s.at[0, 0, h], c_r.at[0, 0, h], here.at_core())
    for h in range(2):
        got = block(1 - here.zl, here.y, here.c, h)
        arrive(got, z_s.at[h], z_r.at[h])
        on_y(got, got, 1, 1, 1, h)
        on_y(got, got, -1, 1, 1, h)
        send(got, got, c_s.at[1, 0, h], c_r.at[1, 0, h], here.at_core())

    def activations():
        for s in range(1, nz):
            t = ((here.zh - s + nz) % nz) * nx + here.x
            for a, (_, dst) in enumerate(arrays):
                arrive(dst.at[t], t1_s.at[s - 1, a], t1_r.at[s - 1, a])
                for sx in range(1, nx):
                    send(dst.at[t], dst.at[t], t2_s.at[sx - 1, s, a], t2_r.at[sx - 1, s, a], here.at_x(sx))

    for k in range(1, far + 1):
        for p in range(2):
            zl = here.zl if p == 0 else 1 - here.zl
            for h in range(2):
                for direction in (1, -1):
                    if not travels(direction, k, h):
                        continue
                    y = (here.y - direction * k + ny) % ny
                    got = block(zl, y, here.c, h)
                    s, r = y_sems(direction)
                    arrive(got, s.at[k - 1, p, h], r.at[k - 1, p, h])
                    on_y(got, got, direction, k + 1, p, h)
                    place = k if direction > 0 else ny - k
                    send(got, got, c_s.at[p, place, h], c_r.at[p, place, h], here.at_core())
        if k == 1:
            activations()
    for sx in range(1, nx):
        for s in range(nz):
            t = ((here.zh - s + nz) % nz) * nx + (here.x - sx + nx) % nx
            for a, (_, dst) in enumerate(arrays):
                arrive(dst.at[t], t2_s.at[sx - 1, s, a], t2_r.at[sx - 1, s, a])
    for p in range(2):
        zl = here.zl if p == 0 else 1 - here.zl
        for place in range(ny):
            y = (here.y - place + ny) % ny
            for h in range(2):
                arrive(block(zl, y, 1 - here.c, h), c_s.at[p, place, h], c_r.at[p, place, h])
    for copy in own:
        copy.wait()
    for copy in sent:
        copy.wait_send()


def gather(dp, tensor, w, x, g):
    ny = dp // (ZL * CORES)
    nz = 4 if tensor == 16 else 2
    nx = tensor // nz
    dma = pltpu.SemaphoreType.DMA
    sems = []
    for dims in ((ny // 2, 2, 2), (ny // 2, 2, 2), (2,), (2, ny, 2), (nz - 1, 2), (nx - 1, nz, 2)):
        sems += [dma(dims), dma(dims)]
    any_spec = pl.BlockSpec(memory_space=pl.ANY)
    return pl.pallas_call(
        functools.partial(gather_kernel, dp, tensor),
        name="gather",
        out_shape=(
            jax.ShapeDtypeStruct((w.shape[0], dp * w.shape[1], w.shape[2]), BF16),
            jax.ShapeDtypeStruct((tensor,) + x.shape, BF16),
            jax.ShapeDtypeStruct((tensor,) + g.shape, BF16),
        ),
        in_specs=[any_spec] * 3,
        out_specs=(any_spec,) * 3,
        scratch_shapes=[dma((3,))] + sems,
        compiler_params=pltpu.CompilerParams(collective_id=0, has_side_effects=True),
    )(w, x, g)


def halves(a):
    high = a.astype(BF16)
    return high, (a - high.astype(F32)).astype(BF16)


def dot(a, b, dims=NN):
    return lax.dot_general(a, b, dims, preferred_element_type=F32)


def product(a, b, dims=NN):
    ah, al = halves(a)
    bh, bl = halves(b)
    side = 0 if dims is NN else 1
    return dot(jnp.concatenate([ah, ah, al], 1), jnp.concatenate([bh, bl, bh], side), dims)


def triangle_product(triangle, a):
    high = a.astype(BF16)
    rest = a - high.astype(F32)
    mid = rest.astype(BF16)
    low = (rest - mid.astype(F32)).astype(BF16)
    return dot(jnp.concatenate([triangle] * 3, 1), jnp.concatenate([high, mid, low], 0))


def unit_inverse(lower, xor):
    inverse = jnp.where(xor == 0, 1.0, 0.0) - jnp.where(xor == 1, lower, 0.0)
    width = 2
    while width < lower.shape[0]:
        between = jnp.where((xor >= width) & (xor < 2 * width), lower, 0.0)
        inverse = inverse - product(product(inverse, between), inverse)
        width *= 2
    return inverse


def head_forward(q, k, v, beta, c_col, c_row, within, strict, xor):
    fading = jnp.where(within, jnp.exp(jnp.where(within, c_col - c_row, 0.0)), 0.0)
    faded_keys = jnp.where(strict, fading * product(k, k, NT), 0.0)
    lower = beta * faded_keys
    inverse = unit_inverse(lower, xor)
    rows = product(inverse, beta * v)
    scores = fading * product(q, k, NT)
    return fading, faded_keys, lower, inverse, rows, scores, product(scores, rows)


def head_backward(q, k, v, beta, fading, faded_keys, lower, inverse, rows, scores, d_out, within, strict):
    d_scores = jnp.where(within, product(d_out, rows, NT), 0.0)
    d_rows = product(scores.T, d_out)
    d_target = product(inverse.T, d_rows)
    d_lower = jnp.where(strict, -product(d_target, rows, NT), 0.0)
    faded = fading * d_scores
    both = beta * fading * d_lower
    dq = product(faded, k)
    dk = product(faded.T, q) + product(both + both.T, k)
    dv = beta * d_target
    spread = d_scores * scores + d_lower * lower
    dc = jnp.sum(spread - spread.T, 1, keepdims=True)
    d_beta = jnp.sum(d_lower * faded_keys + d_target * v, 1, keepdims=True)
    return dq, dk, dv, dc, d_beta


def shifted(a, step, row):
    if step == 0:
        return a
    size = a.shape[0]
    moved = pltpu.roll(a, step % size, 0)
    keep = row >= step if step > 0 else row < size + step
    return jnp.where(keep, moved, 0.0)


def core_kernel(wf_ref, xf_ref, gf_ref, wg_ref, conv_ref, small_ref, core_ref, low_ref, pack_ref, gain_ref, proj, back):
    slots, _, part = xf_ref.shape
    width = wf_ref.shape[2]

    proj[...] = jnp.zeros_like(proj)
    back[...] = jnp.zeros_like(back)

    def contract(i, _):
        rows = pl.ds(pl.multiple_of(i * part, 64), part)
        x, g = xf_ref[i], gf_ref[i]
        for s in range(3):
            proj[:, s * width : (s + 1) * width] += dot(x, wf_ref[s, rows, :])
        proj[:, 3 * width :] += dot(x, wg_ref[rows, :])
        back[...] += dot(g, wf_ref[3, rows, :])
        return 0

    lax.fori_loop(0, slots, contract, 0)

    row = lax.broadcasted_iota(jnp.int32, (LEN, LEN), 0)
    lane = lax.broadcasted_iota(jnp.int32, (LEN, LEN), 1)
    wide_row = lax.broadcasted_iota(jnp.int32, (LEN, width), 0)
    within, strict, xor = row >= lane, row > lane, row ^ lane
    triangle = jnp.where(within, 1.0, 0.0).astype(BF16)
    triangle_t = jnp.where(row <= lane, 1.0, 0.0).astype(BF16)

    rate, bias, gain = small_ref[0:1, :], small_ref[1:2, :], small_ref[2:3, :]
    logits = proj[:, 3 * width :]
    pre = logits + bias
    soft = jnp.maximum(pre, 0.0) + jnp.log1p(jnp.exp(-jnp.abs(pre)))
    strength = 1.0 / (1.0 + jnp.exp(-logits))
    cumulative = triangle_product(triangle, -rate * soft)
    cumulative_t = cumulative.T

    before, gate, active = [], [], []
    for s in range(3):
        p = proj[:, s * width : (s + 1) * width]
        z = jnp.zeros_like(p)
        for i in range(TAPS):
            z = z + conv_ref[s * TAPS + i : s * TAPS + i + 1, :] * shifted(p, TAPS - 1 - i, wide_row)
        sigma = 1.0 / (1.0 + jnp.exp(-z))
        before.append(z)
        gate.append(sigma)
        active.append(z * sigma)

    heads = width // HEAD
    d_active = [[None] * heads for _ in range(3)]
    dc_all = jnp.zeros((LEN, LEN), F32)
    db_all = jnp.zeros((LEN, LEN), F32)
    gain_grad = jnp.zeros((1, HEAD), F32)
    for h in range(heads):
        cut = slice(h * HEAD, (h + 1) * HEAD)
        aq, ak, v = active[0][:, cut], active[1][:, cut], active[2][:, cut]
        nq = lax.rsqrt(jnp.sum(aq * aq, 1, keepdims=True) + 1e-6)
        nk = lax.rsqrt(jnp.sum(ak * ak, 1, keepdims=True) + 1e-6)
        uq, k = aq * nq, ak * nk
        scale = 1.0 / math.sqrt(HEAD)
        q = uq * scale
        beta = strength[:, heads + h : heads + h + 1]
        kept = head_forward(q, k, v, beta, cumulative[:, h : h + 1], cumulative_t[h : h + 1, :], within, strict, xor)
        out = kept[-1]
        r = lax.rsqrt(jnp.mean(out * out, 1, keepdims=True) + 1e-5)
        normed = out * r
        core_ref[:, cut] = (normed * gain).astype(BF16)
        d_core = back[:, cut]
        gain_grad = gain_grad + jnp.sum(d_core * normed, 0, keepdims=True)
        dn = d_core * gain
        d_out = r * (dn - normed * jnp.mean(dn * normed, 1, keepdims=True))
        dq, dk, dv, dc, d_beta = head_backward(q, k, v, beta, *kept[:-1], d_out, within, strict)
        dq = dq * scale
        d_active[0][h] = nq * (dq - uq * jnp.sum(uq * dq, 1, keepdims=True))
        d_active[1][h] = nk * (dk - k * jnp.sum(k * dk, 1, keepdims=True))
        d_active[2][h] = dv
        dc_all = jnp.where(lane == h, dc, dc_all)
        db_all = jnp.where(lane == heads + h, d_beta, db_all)

    pack_ref[...] = jnp.zeros_like(pack_ref)
    gain_ref[...] = jnp.zeros_like(gain_ref)
    gain_ref[0:1, :] = gain_grad
    gate_tiles = slots * pl.cdiv(part, 128) // 2

    for s in range(3):
        z, sigma = before[s], gate[s]
        dz = jnp.concatenate(d_active[s], 1) * (sigma * (1.0 + z * (1.0 - sigma)))
        p = proj[:, s * width : (s + 1) * width]
        dp = jnp.zeros_like(p)
        for i in range(TAPS):
            step = TAPS - 1 - i
            tap = conv_ref[s * TAPS + i : s * TAPS + i + 1, :]
            ahead = shifted(dz, -step, wide_row)
            dp = dp + tap * ahead
            total = jnp.sum(ahead * p, 0, keepdims=True)
            for j in range(width // 128):
                at = j * TAPS + i
                pack_ref[gate_tiles + s, at : at + 1, :] = total[:, j * 128 : (j + 1) * 128]
        low_ref[:, s * width : (s + 1) * width] = dp.astype(BF16)

    d_decay = triangle_product(triangle_t, dc_all)
    d_pre = -rate * d_decay / (1.0 + jnp.exp(-pre))
    pack_ref[gate_tiles + 3, 1:2, :] = jnp.sum(-soft * d_decay, 0, keepdims=True)
    pack_ref[gate_tiles + 3, 2:3, :] = jnp.sum(d_pre, 0, keepdims=True)
    d_logits = (d_pre + db_all * strength * (1.0 - strength)).astype(BF16)
    low_ref[:, 3 * width :] = d_logits
    d_logits_t = d_logits.astype(F32).T[0:16, :].astype(BF16)

    tiles = pl.cdiv(part, 128)

    def gates(i, _):
        for j in range(2):
            grad = dot(d_logits_t, xf_ref[2 * i + j])
            for n in range(tiles):
                at = j * tiles + n
                wide = min(128, part - n * 128)
                piece = grad[0:4, n * 128 : n * 128 + wide]
                pack_ref[i * tiles + at // 2, (at % 2) * 4 : (at % 2) * 4 + 4, 0:wide] = piece
        return 0

    lax.fori_loop(0, slots // 2, gates, 0)


def pack_tiles(dp, slots, part):
    ny = dp // (ZL * CORES)
    gate_tiles = slots * pl.cdiv(part, 128) // 2
    return gate_tiles, pl.cdiv(gate_tiles + 4, ny) * ny


def core(dp, wf, xf, gf, wg, conv, small):
    slots, _, part = xf.shape
    width = wf.shape[2]
    tiles = pack_tiles(dp, slots, part)[1]
    vmem = pl.BlockSpec(memory_space=pltpu.VMEM)
    return pl.pallas_call(
        core_kernel,
        name="core",
        out_shape=(
            jax.ShapeDtypeStruct((LEN, width), BF16),
            jax.ShapeDtypeStruct((LEN, 3 * width + 128), BF16),
            jax.ShapeDtypeStruct((tiles, 8, 128), F32),
            jax.ShapeDtypeStruct((8, 128), F32),
        ),
        in_specs=[vmem] * 6,
        out_specs=(vmem,) * 4,
        scratch_shapes=[pltpu.VMEM((LEN, 3 * width + 128), F32), pltpu.VMEM((LEN, width), F32)],
        compiler_params=pltpu.CompilerParams(vmem_limit_bytes=56 * 2**20),
    )(wf, xf, gf, wg, conv, small)


def reduce_kernel(
    dp, tensor, tiles_before, wf_ref, wg_ref, core_ref, low_ref, pack_ref, gain_ref, out_ref, gin_ref, sum_ref,
    parts, r1, keep, r2, gx, gz, mine, ry, rz, fin, all_sums,
    s1s, s1r, s2s, s2r, gxs, gxr, gzs, gzr, rys, ryr, rzs, rzr, ays, ayr,
):
    here = Place(dp, tensor)
    ny, nz, nx = here.ny, here.nz, here.nx
    part = out_ref.shape[0]
    width = core_ref.shape[1]
    each = pack_ref.shape[0] // ny
    q = here.zl * CORES + here.c

    def at_q(r):
        other = q ^ r
        return here.dp_of(other // CORES, here.y, other % CORES), here.t

    meet(
        [here.at_y(s) for s in range(1, ny)]
        + [at_q(r) for r in range(1, 4)]
        + [here.at_zh(s) for s in range(1, nz)]
        + [here.at_x(s) for s in range(1, nx)]
    )
    sent = []

    def send(src, dst, s, r, where):
        copy = remote(src, dst, s, r, where)
        copy.start()
        sent.append(copy)

    def arrive(dst, s, r):
        remote(dst, dst, s, r, here.at_core()).wait_recv()

    def back_of(step, size, now):
        return (now - step + size) % size

    gx[here.x] = gain_ref[...]
    for s in range(1, nx):
        send(gain_ref, gx.at[here.x], gxs.at[s - 1], gxr.at[s - 1], here.at_x(s))

    def first(a, build):
        def piece(i, _):
            sx, zh = (i // nz + 1) % nx, i % nz
            x = (here.x + sx) % nx
            t = zh * nx + x
            parts[a, t] = build(pl.ds(pl.multiple_of(t * part, 64), part)).astype(BF16)

            @pl.when(sx != 0)
            def _():
                remote(parts.at[a, t], r1.at[a, sx, zh], s1s.at[a, sx, zh], s1r.at[a, sx, zh], (here.d, here.zh * nx + x)).start()

            return 0

        lax.fori_loop(0, nx * nz, piece, 0)

    def second(a):
        for sz in [*range(1, nz), 0]:
            zh = (here.zh + sz) % nz
            total = parts[a, zh * nx + here.x].astype(F32)
            for sx in range(1, nx):
                arrive(r1.at[a, sx, zh], s1s.at[a, sx, zh], s1r.at[a, sx, zh])
                total = total + r1[a, sx, zh].astype(F32)
            if sz:
                mine[a, sz] = total.astype(BF16)
                send(mine.at[a, sz], r2.at[a, sz], s2s.at[a, sz], s2r.at[a, sz], here.at_zh(sz))
            else:
                keep[a] = total

    def last(a, ref):
        total = keep[a]
        for sz in range(1, nz):
            arrive(r2.at[a, sz], s2s.at[a, sz], s2r.at[a, sz])
            total = total + r2[a, sz].astype(F32)
        ref[...] = total.astype(BF16)

    first(0, lambda rows: dot(wf_ref[3, rows, :], core_ref[...], NT))

    for s in range(1, nx):
        arrive(gx.at[back_of(s, nx, here.x)], gxs.at[s - 1], gxr.at[s - 1])
    gz[here.zh] = sum(gx[i] for i in range(nx))
    for s in range(1, nz):
        send(gz.at[here.zh], gz.at[here.zh], gzs.at[s - 1], gzr.at[s - 1], here.at_zh(s))

    def grad_in(rows):
        total = dot(wg_ref[rows, :], low_ref[:, 3 * width :], NT)
        for s in range(3):
            total = total + dot(wf_ref[s, rows, :], low_ref[:, s * width : (s + 1) * width], NT)
        return total

    first(1, grad_in)

    for s in range(1, nz):
        arrive(gz.at[back_of(s, nz, here.zh)], gzs.at[s - 1], gzr.at[s - 1])
    sum_ref[...] = pack_ref[...]
    gain_at = tiles_before + 3
    sum_ref[gain_at, 0:1, :] = sum(gz[i, 0:1, :] for i in range(nz))
    own = pl.ds(here.y * each, each)
    mark = len(sent)
    for s in range(1, ny):
        there = (here.y + s) % ny
        send(sum_ref.at[pl.ds(there * each, each)], ry.at[here.y], rys.at[s - 1], ryr.at[s - 1], here.at_y(s))
    ry[here.y] = sum_ref[own]
    leaving, sent[mark:] = sent[mark:], []

    second(0)

    for s in range(1, ny):
        arrive(ry.at[back_of(s, ny, here.y)], rys.at[s - 1], ryr.at[s - 1])
    rz[q] = sum(ry[i] for i in range(ny))
    for r in range(1, 4):
        send(rz.at[q], rz.at[q], rzs.at[r - 1], rzr.at[r - 1], at_q(r))

    last(0, out_ref)
    second(1)

    for r in range(1, 4):
        arrive(rz.at[q ^ r], rzs.at[r - 1], rzr.at[r - 1])
    fin[...] = sum(rz[i] for i in range(4))
    for s in range(1, ny):
        send(fin, all_sums.at[here.y], ays.at[s - 1], ayr.at[s - 1], here.at_y(s))
    all_sums[here.y] = fin[...]
    for s in range(1, ny):
        arrive(all_sums.at[back_of(s, ny, here.y)], ays.at[s - 1], ayr.at[s - 1])
    for copy in leaving:
        copy.wait_send()
    for i in range(ny):
        sum_ref[i * each : (i + 1) * each] = all_sums[i]

    last(1, gin_ref)

    def finished(i, _):
        sx, zh = i // nz + 1, i % nz
        for a in range(2):
            remote(parts.at[a, 0], r1.at[a, sx, zh], s1s.at[a, sx, zh], s1r.at[a, sx, zh], here.at_core()).wait_send()
        return 0

    lax.fori_loop(0, (nx - 1) * nz, finished, 0)
    for copy in sent:
        copy.wait_send()


def reduce(dp, tensor, wf, wg, core_low, low, pack, gain):
    ny = dp // (ZL * CORES)
    nz = 4 if tensor == 16 else 2
    nx = tensor // nz
    part = wf.shape[1] // tensor
    each = pack.shape[0] // ny
    vmem = pl.BlockSpec(memory_space=pltpu.VMEM)
    dma = pltpu.SemaphoreType.DMA
    sems = []
    for dims in ((2, nx, nz), (2, nz), (nx - 1,), (nz - 1,), (ny - 1,), (3,), (ny - 1,)):
        sems += [dma(dims), dma(dims)]
    gate_tiles = pack_tiles(dp, tensor, part)[0]
    return pl.pallas_call(
        functools.partial(reduce_kernel, dp, tensor, gate_tiles),
        name="reduce",
        out_shape=(
            jax.ShapeDtypeStruct((part, LEN), BF16),
            jax.ShapeDtypeStruct((part, LEN), BF16),
            jax.ShapeDtypeStruct(pack.shape, F32),
        ),
        in_specs=[vmem] * 6,
        out_specs=(vmem,) * 3,
        scratch_shapes=[
            pltpu.VMEM((2, tensor, part, LEN), BF16),
            pltpu.VMEM((2, nx, nz, part, LEN), BF16),
            pltpu.VMEM((2, part, LEN), F32),
            pltpu.VMEM((2, nz, part, LEN), BF16),
            pltpu.VMEM((nx, 8, 128), F32),
            pltpu.VMEM((nz, 8, 128), F32),
            pltpu.VMEM((2, nz, part, LEN), BF16),
            pltpu.VMEM((ny, each, 8, 128), F32),
            pltpu.VMEM((4, each, 8, 128), F32),
            pltpu.VMEM((each, 8, 128), F32),
            pltpu.VMEM((ny, each, 8, 128), F32),
        ]
        + sems,
        compiler_params=pltpu.CompilerParams(collective_id=1, has_side_effects=True, vmem_limit_bytes=56 * 2**20),
    )(wf, wg, core_low, low, pack, gain)


def on_device(dp, tensor, inputs, w_qkv, w_gates, conv_weight, decay_rate, gate_bias, norm_gain, w_out, grad_out):
    part, slots = inputs.shape[2], tensor
    heads = decay_rate.shape[0]
    width = w_qkv.shape[2]
    shards = jnp.concatenate([w_qkv, w_out.T[None]], 0)
    wg = jnp.pad(jnp.moveaxis(w_gates, 0, 1).reshape(-1, 2 * heads), ((0, 0), (0, 128 - 2 * heads)))
    small = jnp.stack([jnp.pad(decay_rate, (0, 128 - heads)), jnp.pad(gate_bias, (0, 128 - heads)), norm_gain])
    small = jnp.pad(small, ((0, 5), (0, 0)))
    conv = conv_weight.reshape(3 * TAPS, width)
    wf, xf, gf = gather(dp, tensor, shards, inputs[0], grad_out[0])
    core_low, low, pack, gain = core(dp, wf, xf, gf, wg, conv, small)
    out, grad_in, total = reduce(dp, tensor, wf, wg, core_low, low, pack, gain)
    tiles = pl.cdiv(part, 128)
    count = pack_tiles(dp, slots, part)[0]
    gates = total[:count].reshape(slots, tiles, 4, 128)[:, :, : 2 * heads]
    gates = gates.transpose(2, 0, 1, 3).reshape(2, heads, slots, tiles * 128)[..., :part]
    grad_gates = gates.reshape(2, heads, slots * part).transpose(0, 2, 1)
    taps = total[count : count + 3].reshape(3, width // 128, TAPS, 128)
    grad_conv = taps.transpose(0, 2, 1, 3).reshape(3, TAPS, width)
    rest = total[count + 3]
    return (out.T[None], grad_in.T[None], grad_gates, grad_conv, rest[1, :heads], rest[2, :heads], rest[0])


def solution(mesh):
    dp, tensor = mesh.shape["dp"], mesh.shape["tensor"]
    return jax.shard_map(
        functools.partial(on_device, dp, tensor),
        mesh=mesh,
        in_specs=(
            P("dp", None, "tensor"),
            P(None, "dp", "tensor"),
            P(None, None, "tensor"),
            P(None, None, "tensor"),
            P("tensor"),
            P("tensor"),
            P(),
            P("tensor", "dp"),
            P("dp", None, "tensor"),
        ),
        out_specs=(
            P("dp", None, "tensor"),
            P("dp", None, "tensor"),
            P(None, None, "tensor"),
            P(None, None, "tensor"),
            P("tensor"),
            P("tensor"),
            P(),
        ),
        check_vma=False,
    )
```

```python
import functools
import math

import jax
import jax.numpy as jnp
from jax import lax
from jax.experimental import pallas as pl
from jax.experimental.pallas import tpu as pltpu
from jax.sharding import PartitionSpec as P

MESH = pl.DeviceIdType.MESH
F32, BF16 = jnp.float32, jnp.bfloat16
LEN = 128
HEAD = 128
TAPS = 4
CORES = 2
ZL = 2
NN = (((1,), (0,)), ((), ()))
NT = (((1,), (1,)), ((), ()))


class Place:
    def __init__(self, dp, tensor):
        self.ny = dp // (ZL * CORES)
        self.nz = 4 if tensor == 16 else 2
        self.nx = tensor // self.nz
        d, t = lax.axis_index("dp"), lax.axis_index("tensor")
        self.d, self.t = d, t
        self.zl = d // (self.ny * CORES)
        self.y = (d // CORES) % self.ny
        self.c = d % CORES
        self.zh = t // self.nx
        self.x = t % self.nx

    def dp_of(self, zl, y, c):
        return zl * (self.ny * CORES) + y * CORES + c

    def at_y(self, step):
        return self.dp_of(self.zl, (self.y + step + self.ny) % self.ny, self.c), self.t

    def at_z(self):
        return self.dp_of(1 - self.zl, self.y, self.c), self.t

    def at_core(self):
        return self.dp_of(self.zl, self.y, 1 - self.c), self.t

    def at_zh(self, step):
        return self.d, ((self.zh + step + self.nz) % self.nz) * self.nx + self.x

    def at_x(self, step):
        return self.d, self.zh * self.nx + (self.x + step + self.nx) % self.nx


def remote(src, dst, send, recv, where):
    return pltpu.make_async_remote_copy(
        src_ref=src, dst_ref=dst, send_sem=send, recv_sem=recv, device_id=where, device_id_type=MESH
    )


def meet(peers):
    barrier = pltpu.get_barrier_semaphore()
    for where in peers:
        pl.semaphore_signal(barrier, inc=1, device_id=where, device_id_type=MESH)
    pl.semaphore_wait(barrier, len(peers))


def halves(a):
    high = a.astype(BF16)
    return high, (a - high.astype(F32)).astype(BF16)


def dot(a, b, dims=NN):
    return lax.dot_general(a, b, dims, preferred_element_type=F32)


def product(a, b, dims=NN):
    ah, al = halves(a)
    bh, bl = halves(b)
    side = 0 if dims is NN else 1
    return dot(jnp.concatenate([ah, ah, al], 1), jnp.concatenate([bh, bl, bh], side), dims)


def triangle_product(triangle, a):
    high = a.astype(BF16)
    rest = a - high.astype(F32)
    mid = rest.astype(BF16)
    low = (rest - mid.astype(F32)).astype(BF16)
    return dot(jnp.concatenate([triangle] * 3, 1), jnp.concatenate([high, mid, low], 0))


def unit_inverse(lower, xor):
    inverse = jnp.where(xor == 0, 1.0, 0.0) - jnp.where(xor == 1, lower, 0.0)
    width = 2
    while width < lower.shape[0]:
        between = jnp.where((xor >= width) & (xor < 2 * width), lower, 0.0)
        inverse = inverse - product(product(inverse, between), inverse)
        width *= 2
    return inverse


def head_forward(q, k, v, beta, c_col, c_row, within, strict, xor):
    fading = jnp.where(within, jnp.exp(jnp.where(within, c_col - c_row, 0.0)), 0.0)
    faded_keys = jnp.where(strict, fading * product(k, k, NT), 0.0)
    lower = beta * faded_keys
    inverse = unit_inverse(lower, xor)
    rows = product(inverse, beta * v)
    scores = fading * product(q, k, NT)
    return fading, faded_keys, lower, inverse, rows, scores, product(scores, rows)


def head_backward(q, k, v, beta, fading, faded_keys, lower, inverse, rows, scores, d_out, within, strict):
    d_scores = jnp.where(within, product(d_out, rows, NT), 0.0)
    d_rows = product(scores.T, d_out)
    d_target = product(inverse.T, d_rows)
    d_lower = jnp.where(strict, -product(d_target, rows, NT), 0.0)
    faded = fading * d_scores
    both = beta * fading * d_lower
    dq = product(faded, k)
    dk = product(faded.T, q) + product(both + both.T, k)
    dv = beta * d_target
    spread = d_scores * scores + d_lower * lower
    dc = jnp.sum(spread - spread.T, 1, keepdims=True)
    d_beta = jnp.sum(d_lower * faded_keys + d_target * v, 1, keepdims=True)
    return dq, dk, dv, dc, d_beta


def shifted(a, step, row):
    if step == 0:
        return a
    size = a.shape[0]
    moved = pltpu.roll(a, step % size, 0)
    keep = row >= step if step > 0 else row < size + step
    return jnp.where(keep, moved, 0.0)


class Stream:
    def __init__(self, here, early, mine, full, sems):
        self.here, self.early = here, early
        self.far = here.ny // 2
        self.shard = mine.shape[-2]
        self.half = self.shard // 2
        self.mine, self.full = mine, full
        self.yp, self.ym, self.z, self.c = (sems[i : i + 2] for i in (0, 2, 4, 6))
        self.sent = []

    def rows(self, ref, start, size):
        return ref.at[:, pl.ds(start, size), :] if len(ref.shape) == 3 else ref.at[pl.ds(start, size), :]

    def block(self, p, place, h, other_core=False):
        here = self.here
        zl = here.zl if p == 0 else 1 - here.zl
        c = 1 - here.c if other_core else here.c
        d = here.dp_of(zl, (here.y - place + here.ny) % here.ny, c)
        return self.rows(self.full, pl.multiple_of(d * self.shard + h * self.half, 16), self.half)

    def send(self, src, dst, sems, index, where):
        copy = remote(src, dst, sems[0].at[index], sems[1].at[index], where)
        copy.start()
        self.sent.append(copy)

    def arrive(self, dst, sems, index):
        remote(dst, dst, sems[0].at[index], sems[1].at[index], self.here.at_core()).wait_recv()

    def travels(self, direction, k, h):
        return k < self.far or (k == self.far and h == (0 if direction > 0 else 1))

    def along_y(self, src, dst, direction, k, p, h):
        if self.travels(direction, k, h):
            self.send(src, dst, self.yp if direction > 0 else self.ym, (k - 1, p, h), self.here.at_y(direction))

    def to_core(self, src, dst, p, place, h):
        self.send(src, dst, self.c, (p, place, h), self.here.at_core())

    def start(self):
        here = self.here
        for h in range(2):
            src, dst = self.rows(self.mine, h * self.half, self.half), self.block(0, 0, h)
            self.along_y(src, dst, 1, 1, 0, h)
            self.along_y(src, dst, -1, 1, 0, h)
            self.send(src, dst, self.z, (0, h), here.at_z())

    def own_to_core(self):
        for h in range(2):
            self.to_core(self.rows(self.mine, h * self.half, self.half), self.block(0, 0, h), 0, 0, h)

    def places(self, k):
        far, ny = self.far, self.here.ny
        return [k] if k in (0, far) else [k, ny - k]

    def from_z(self, k):
        for place in self.places(k):
            for h in range(2):
                got = self.block(1, place, h)
                self.arrive(got, self.z, (place, h))
                if self.early:
                    self.along_y(got, got, 1, 1, 1, h)
                    self.along_y(got, got, -1, 1, 1, h)
                self.to_core(got, got, 1, place, h)

    def from_y(self, k):
        here = self.here
        for p in range(2 if self.early else 1):
            for h in range(2):
                for direction in (1, -1):
                    if not self.travels(direction, k, h):
                        continue
                    place = k if direction > 0 else here.ny - k
                    got = self.block(p, place, h)
                    self.arrive(got, self.yp if direction > 0 else self.ym, (k - 1, p, h))
                    self.along_y(got, got, direction, k + 1, p, h)
                    if not self.early:
                        self.send(got, got, self.z, (place, h), here.at_z())
                    self.to_core(got, got, p, place, h)

    def from_core(self, k):
        for p in range(2):
            for place in self.places(k):
                for h in range(2):
                    self.arrive(self.block(p, place, h, True), self.c, (p, place, h))

    def finish(self):
        for copy in self.sent:
            copy.wait_send()


def stream_sems(ny, early):
    dma = pltpu.SemaphoreType.DMA
    sems = []
    for dims in ((ny // 2, 2 if early else 1, 2),) * 2 + ((1 if early else ny, 2), (2, ny, 2)):
        sems += [dma(dims), dma(dims)]
    return sems


def layer_kernel(
    dp, tensor, w_ref, wo_ref, x_ref, g_ref, wg_ref, conv_ref, rate_ref, bias_ref, gain_ref, res_ref, sum_ref, *scratch
):
    scratch = list(scratch)

    def take(n):
        out = scratch[:n]
        del scratch[:n]
        return out

    wf, wof, xt, gt, xr, gr, wg16, gcol, proj, back, core_low, low, pack = take(13)
    parts, r1, keep, r2, gx, gz, mine, ry, rz, fin, all_sums = take(11)
    own_sem, t1s, t1r, t2s, t2r, s1s, s1r, s2s, s2r, gxs, gxr, gzs, gzr, rys, ryr, rzs, rzr, ays, ayr = take(19)
    here = Place(dp, tensor)
    ny, nz, nx = here.ny, here.nz, here.nx
    far = ny // 2
    part = x_ref.shape[0]
    width = w_ref.shape[2]
    heads = width // HEAD
    each = pack.shape[0] // ny
    gate_tiles = xt.shape[0] // 256
    q = here.zl * CORES + here.c

    qk = Stream(here, True, w_ref.at[pl.ds(0, 2)], wf.at[pl.ds(0, 2)], take(8))
    vv = Stream(here, False, w_ref.at[2], wf.at[2], take(8))
    oo = Stream(here, False, wo_ref, wof, take(8))
    sent = []

    def at_q(r):
        other = q ^ r
        return here.dp_of(other // CORES, here.y, other % CORES), here.t

    def send(src, dst, s, r, where):
        copy = remote(src, dst, s, r, where)
        copy.start()
        sent.append(copy)

    def arrive(dst, s, r):
        remote(dst, dst, s, r, here.at_core()).wait_recv()

    def back_of(step, size, now):
        return (now - step + size) % size

    def slot(ref, t):
        return ref.at[pl.ds(pl.multiple_of(t * part, 16), part), :]

    meet(
        [here.at_y(s) for s in range(1, ny)]
        + [at_q(r) for r in range(1, 4)]
        + [here.at_zh(s) for s in range(1, nz)]
        + [here.at_x(s) for s in range(1, nx)]
    )

    arrays = ((x_ref, xt), (g_ref, gt))
    qk.start()
    vv.start()
    for a, (src, dst) in enumerate(arrays):
        for s in range(1, nz):
            send(src, slot(dst, here.t), t1s.at[s - 1, a], t1r.at[s - 1, a], here.at_zh(s))
        for s in range(1, nx):
            send(src, slot(dst, here.t), t2s.at[s - 1, 0, a], t2r.at[s - 1, 0, a], here.at_x(s))
    qk.own_to_core()
    vv.own_to_core()
    mine_rows = pl.ds(pl.multiple_of(here.d * w_ref.shape[1], 16), w_ref.shape[1])
    own = [
        pltpu.make_async_copy(x_ref, slot(xt, here.t), own_sem.at[0]),
        pltpu.make_async_copy(g_ref, slot(gt, here.t), own_sem.at[1]),
        pltpu.make_async_copy(w_ref, wf.at[:, mine_rows, :], own_sem.at[2]),
        pltpu.make_async_copy(wo_ref, wof.at[mine_rows, :], own_sem.at[3]),
    ]
    for copy in own:
        copy.start()

    proj[...] = jnp.zeros_like(proj)
    back[...] = jnp.zeros_like(back)
    pack[...] = jnp.zeros_like(pack)
    wide = wg_ref[...].astype(F32)
    wg16[...] = jnp.concatenate([wide[0], wide[1], jnp.zeros((16 - 2 * heads, wide.shape[2]), F32)], 0).astype(BF16)

    def column(i, _):
        at = pl.ds(pl.multiple_of(i * 128, 128), 128)
        tall = jnp.concatenate([wg16[:, at].astype(F32), jnp.zeros((112, 128), F32)], 0)
        gcol[at, :] = tall.T.astype(BF16)
        return 0

    lax.fori_loop(0, xt.shape[0] // 128, column, 0)
    qk.from_z(0)
    for copy in own:
        copy.wait()

    def spread():
        for a, (_, dst) in enumerate(arrays):
            for s in range(1, nz):
                got = slot(dst, back_of(s, nz, here.zh) * nx + here.x)
                arrive(got, t1s.at[s - 1, a], t1r.at[s - 1, a])
                for sx in range(1, nx):
                    send(got, got, t2s.at[sx - 1, s, a], t2r.at[sx - 1, s, a], here.at_x(sx))

    def landed(a, turned):
        dst = arrays[a][1]
        for s in range(nz):
            for sx in range(1, nx):
                got = slot(dst, back_of(s, nz, here.zh) * nx + back_of(sx, nx, here.x))
                arrive(got, t2s.at[sx - 1, s, a], t2r.at[sx - 1, s, a])

        def turn(t, _):
            turned[t] = dst[pl.ds(pl.multiple_of(t * part, 16), part), :].T
            return 0

        lax.fori_loop(0, tensor, turn, 0)

    def contract(k):
        qk.from_core(k)
        vv.from_core(k)
        ways = len(qk.places(k))

        def term(i, _):
            zl = jnp.where(i // ways == 0, here.zl, 1 - here.zl)
            step = jnp.where(i % ways == 0, k, ny - k)
            t = zl * ny + (here.y - step + ny) % ny
            rows = pl.ds(pl.multiple_of(t * part, 16), part)
            x = xr[t]
            for s in range(3):
                proj[:, s * width : (s + 1) * width] += dot(x, wf[s, rows, :])
            return 0

        lax.fori_loop(0, 2 * ways, term, 0)

    todo = []
    turned_x = turned_g = False
    for k in range(1, far + 1):
        if k == far:
            oo.start()
            oo.own_to_core()
        qk.from_y(k)
        vv.from_y(k)
        vv.from_z(k - 1)
        todo.append(k - 1)
        if k == 1:
            spread()
        if k >= 2:
            if not turned_x:
                landed(0, xr)
                turned_x = True
            for j in todo:
                contract(j)
            todo = []
        if k >= 3 and not turned_g:
            landed(1, gr)
            turned_g = True
    if not turned_x:
        landed(0, xr)
    logits_t = dot(wg16[...], xt[...])
    vv.from_z(far)
    for j in [*todo, far]:
        contract(j)
    if not turned_g:
        landed(1, gr)
    oo.from_y(1)
    oo.from_z(0)

    row = lax.broadcasted_iota(jnp.int32, (LEN, LEN), 0)
    lane = lax.broadcasted_iota(jnp.int32, (LEN, LEN), 1)
    wide_row = lax.broadcasted_iota(jnp.int32, (LEN, width), 0)
    within, strict, xor = row >= lane, row > lane, row ^ lane
    triangle = jnp.where(within, 1.0, 0.0).astype(BF16)
    triangle_t = jnp.where(row <= lane, 1.0, 0.0).astype(BF16)
    lane_1 = lax.broadcasted_iota(jnp.int32, (1, LEN), 1)
    rate = sum(jnp.where(lane_1 == h, rate_ref[h], 0.0) for h in range(heads))
    bias = sum(jnp.where(lane_1 == h, bias_ref[h], 0.0) for h in range(heads))
    gain = gain_ref[...]

    logits = jnp.concatenate([logits_t, jnp.zeros((LEN - 16, LEN), F32)], 0).T
    pre = logits + bias
    soft = jnp.maximum(pre, 0.0) + jnp.log1p(jnp.exp(-jnp.abs(pre)))
    strength = 1.0 / (1.0 + jnp.exp(-logits))
    cumulative = triangle_product(triangle, -rate * soft)
    cumulative_t = cumulative.T

    before, gate, active = [], [], []
    for s in range(3):
        p = proj[:, s * width : (s + 1) * width]
        z = jnp.zeros_like(p)
        for i in range(TAPS):
            z = z + conv_ref[s, i : i + 1, :] * shifted(p, TAPS - 1 - i, wide_row)
        sigma = 1.0 / (1.0 + jnp.exp(-z))
        before.append(z)
        gate.append(sigma)
        active.append(z * sigma)

    for k in range(2, far + 1):
        oo.from_y(k)
        oo.from_z(k - 1)

    scale = 1.0 / math.sqrt(HEAD)
    kept = []
    for h in range(heads):
        cut = slice(h * HEAD, (h + 1) * HEAD)
        aq, ak, v = active[0][:, cut], active[1][:, cut], active[2][:, cut]
        nq = lax.rsqrt(jnp.sum(aq * aq, 1, keepdims=True) + 1e-6)
        nk = lax.rsqrt(jnp.sum(ak * ak, 1, keepdims=True) + 1e-6)
        uq, k = aq * nq, ak * nk
        beta = strength[:, heads + h : heads + h + 1]
        held = head_forward(uq * scale, k, v, beta, cumulative[:, h : h + 1], cumulative_t[h : h + 1, :], within, strict, xor)
        out = held[-1]
        r = lax.rsqrt(jnp.mean(out * out, 1, keepdims=True) + 1e-5)
        normed = out * r
        core_low[:, cut] = (normed * gain).astype(BF16)
        kept.append((nq, nk, uq, k, v, beta, held[:-1], r, normed))

    oo.from_z(far)
    for k in range(far + 1):
        oo.from_core(k)

    def first(a, build):
        def piece(i, _):
            sx, zh = (i // nz + 1) % nx, i % nz
            x = (here.x + sx) % nx
            t = zh * nx + x
            parts[a, t] = build(pl.ds(pl.multiple_of(t * part, 16), part)).astype(BF16)

            @pl.when(sx != 0)
            def _():
                remote(parts.at[a, t], r1.at[a, sx, zh], s1s.at[a, sx, zh], s1r.at[a, sx, zh], (here.d, here.zh * nx + x)).start()

            return 0

        lax.fori_loop(0, nx * nz, piece, 0)

    def second(a):
        for sz in [*range(1, nz), 0]:
            zh = (here.zh + sz) % nz
            total = parts[a, zh * nx + here.x].astype(F32)
            for sx in range(1, nx):
                arrive(r1.at[a, sx, zh], s1s.at[a, sx, zh], s1r.at[a, sx, zh])
                total = total + r1[a, sx, zh].astype(F32)
            if sz:
                mine[a, sz] = total.astype(BF16)
                send(mine.at[a, sz], r2.at[a, sz], s2s.at[a, sz], s2r.at[a, sz], here.at_zh(sz))
            else:
                keep[a] = total

    def last(a):
        total = keep[a]
        for sz in range(1, nz):
            arrive(r2.at[a, sz], s2s.at[a, sz], s2r.at[a, sz])
            total = total + r2[a, sz].astype(F32)
        res_ref[a] = total.astype(BF16)

    first(0, lambda rows: dot(wof[rows, :], core_low[...], NT))

    def back_term(t, _):
        back[...] += dot(gr[t], wof[pl.ds(pl.multiple_of(t * part, 16), part), :])
        return 0

    lax.fori_loop(0, tensor, back_term, 0)

    gain_grad = jnp.zeros((1, HEAD), F32)
    for h in range(heads):
        gain_grad = gain_grad + jnp.sum(back[:, h * HEAD : (h + 1) * HEAD] * kept[h][-1], 0, keepdims=True)
    gx[here.x] = jnp.concatenate([gain_grad, jnp.zeros((7, HEAD), F32)], 0)
    for s in range(1, nx):
        send(gx.at[here.x], gx.at[here.x], gxs.at[s - 1], gxr.at[s - 1], here.at_x(s))

    d_active = [[None] * heads for _ in range(3)]
    dc_all = jnp.zeros((LEN, LEN), F32)
    db_all = jnp.zeros((LEN, LEN), F32)
    for h in range(heads):
        nq, nk, uq, k, v, beta, held, r, normed = kept[h]
        dn = back[:, h * HEAD : (h + 1) * HEAD] * gain
        d_out = r * (dn - normed * jnp.mean(dn * normed, 1, keepdims=True))
        dq, dk, dv, dc, d_beta = head_backward(uq * scale, k, v, beta, *held, d_out, within, strict)
        dq = dq * scale
        d_active[0][h] = nq * (dq - uq * jnp.sum(uq * dq, 1, keepdims=True))
        d_active[1][h] = nk * (dk - k * jnp.sum(k * dk, 1, keepdims=True))
        d_active[2][h] = dv
        dc_all = jnp.where(lane == h, dc, dc_all)
        db_all = jnp.where(lane == heads + h, d_beta, db_all)

    for s in range(1, nx):
        arrive(gx.at[back_of(s, nx, here.x)], gxs.at[s - 1], gxr.at[s - 1])
    gz[here.zh] = sum(gx[i] for i in range(nx))
    for s in range(1, nz):
        send(gz.at[here.zh], gz.at[here.zh], gzs.at[s - 1], gzr.at[s - 1], here.at_zh(s))

    d_decay = triangle_product(triangle_t, dc_all)
    d_pre = -rate * d_decay / (1.0 + jnp.exp(-pre))
    pack[gate_tiles + 3, 1:2, :] = jnp.sum(-soft * d_decay, 0, keepdims=True)
    pack[gate_tiles + 3, 2:3, :] = jnp.sum(d_pre, 0, keepdims=True)
    d_logits = (d_pre + db_all * strength * (1.0 - strength)).astype(BF16)
    low[:, 3 * width :] = d_logits
    d_logits_t = d_logits.astype(F32).T[0:16, :].astype(BF16)

    for s in range(3):
        z, sigma = before[s], gate[s]
        dz = jnp.concatenate(d_active[s], 1) * (sigma * (1.0 + z * (1.0 - sigma)))
        p = proj[:, s * width : (s + 1) * width]
        dp_s = jnp.zeros_like(p)
        for i in range(TAPS):
            ahead = shifted(dz, i + 1 - TAPS, wide_row)
            dp_s = dp_s + conv_ref[s, i : i + 1, :] * ahead
            total = jnp.sum(ahead * p, 0, keepdims=True)
            for j in range(width // 128):
                at = j * TAPS + i
                pack[gate_tiles + s, at : at + 1, :] = total[:, j * 128 : (j + 1) * 128]
        low[:, s * width : (s + 1) * width] = dp_s.astype(BF16)

    def grad_in(rows):
        total = dot(gcol[rows, :], low[:, 3 * width :], NT)
        for s in range(3):
            total = total + dot(wf[s, rows, :], low[:, s * width : (s + 1) * width], NT)
        return total

    first(1, grad_in)

    def gates(i, _):
        grad = dot(d_logits_t, xt[pl.ds(pl.multiple_of(i * 256, 256), 256), :], NT)
        pack[i, 0:4, :] = grad[0:4, 0:128]
        pack[i, 4:8, :] = grad[0:4, 128:256]
        return 0

    lax.fori_loop(0, gate_tiles, gates, 0)

    for s in range(1, nz):
        arrive(gz.at[back_of(s, nz, here.zh)], gzs.at[s - 1], gzr.at[s - 1])
    pack[gate_tiles + 3, 0:1, :] = sum(gz[i, 0:1, :] for i in range(nz))
    for s in range(1, ny):
        there = (here.y + s) % ny
        send(pack.at[pl.ds(there * each, each)], ry.at[here.y], rys.at[s - 1], ryr.at[s - 1], here.at_y(s))
    ry[here.y] = pack[pl.ds(here.y * each, each)]

    second(0)

    for s in range(1, ny):
        arrive(ry.at[back_of(s, ny, here.y)], rys.at[s - 1], ryr.at[s - 1])
    rz[q] = sum(ry[i] for i in range(ny))
    for r in range(1, 4):
        send(rz.at[q], rz.at[q], rzs.at[r - 1], rzr.at[r - 1], at_q(r))

    last(0)
    second(1)

    for r in range(1, 4):
        arrive(rz.at[q ^ r], rzs.at[r - 1], rzr.at[r - 1])
    fin[...] = sum(rz[i] for i in range(4))
    for s in range(1, ny):
        send(fin, all_sums.at[here.y], ays.at[s - 1], ayr.at[s - 1], here.at_y(s))
    all_sums[here.y] = fin[...]
    for s in range(1, ny):
        arrive(all_sums.at[back_of(s, ny, here.y)], ays.at[s - 1], ayr.at[s - 1])
    for i in range(ny):
        sum_ref[i * each : (i + 1) * each] = all_sums[i]

    last(1)

    def finished(i, _):
        sx, zh = i // nz + 1, i % nz
        for a in range(2):
            remote(parts.at[a, 0], r1.at[a, sx, zh], s1s.at[a, sx, zh], s1r.at[a, sx, zh], here.at_core()).wait_send()
        return 0

    lax.fori_loop(0, (nx - 1) * nz, finished, 0)
    for stream in (qk, vv, oo):
        stream.finish()
    for copy in sent:
        copy.wait_send()


def layer(dp, tensor, w, wo, x, g, wg, conv, rate, bias, gain):
    ny = dp // (ZL * CORES)
    nz = 4 if tensor == 16 else 2
    nx = tensor // nz
    part = x.shape[0]
    model, width = part * tensor, w.shape[2]
    tiles = pl.cdiv(model // 256 + 4, ny) * ny
    each = tiles // ny
    any_spec = pl.BlockSpec(memory_space=pl.ANY)
    vmem = pl.BlockSpec(memory_space=pltpu.VMEM)
    smem = pl.BlockSpec(memory_space=pltpu.SMEM)
    dma = pltpu.SemaphoreType.DMA
    sems = [dma((4,))]
    for dims in (
        (nz - 1, 2), (nx - 1, nz, 2), (2, nx, nz), (2, nz), (nx - 1,), (nz - 1,), (ny - 1,), (3,), (ny - 1,),
    ):
        sems += [dma(dims), dma(dims)]
    sems += stream_sems(ny, True) + stream_sems(ny, False) + stream_sems(ny, False)
    return pl.pallas_call(
        functools.partial(layer_kernel, dp, tensor),
        name="layer",
        out_shape=(jax.ShapeDtypeStruct((2, part, LEN), BF16), jax.ShapeDtypeStruct((tiles, 8, 128), F32)),
        in_specs=[any_spec] * 4 + [vmem] * 2 + [smem] * 2 + [vmem],
        out_specs=(vmem,) * 2,
        scratch_shapes=[
            pltpu.VMEM((3, model, width), BF16),
            pltpu.VMEM((model, width), BF16),
            pltpu.VMEM((model, LEN), BF16),
            pltpu.VMEM((model, LEN), BF16),
            pltpu.VMEM((tensor, LEN, part), BF16),
            pltpu.VMEM((tensor, LEN, part), BF16),
            pltpu.VMEM((16, model), BF16),
            pltpu.VMEM((model, 128), BF16),
            pltpu.VMEM((LEN, 3 * width), F32),
            pltpu.VMEM((LEN, width), F32),
            pltpu.VMEM((LEN, width), BF16),
            pltpu.VMEM((LEN, 3 * width + 128), BF16),
            pltpu.VMEM((tiles, 8, 128), F32),
            pltpu.VMEM((2, tensor, part, LEN), BF16),
            pltpu.VMEM((2, nx, nz, part, LEN), BF16),
            pltpu.VMEM((2, part, LEN), F32),
            pltpu.VMEM((2, nz, part, LEN), BF16),
            pltpu.VMEM((nx, 8, 128), F32),
            pltpu.VMEM((nz, 8, 128), F32),
            pltpu.VMEM((2, nz, part, LEN), BF16),
            pltpu.VMEM((ny, each, 8, 128), F32),
            pltpu.VMEM((4, each, 8, 128), F32),
            pltpu.VMEM((each, 8, 128), F32),
            pltpu.VMEM((ny, each, 8, 128), F32),
        ]
        + sems,
        compiler_params=pltpu.CompilerParams(collective_id=0, has_side_effects=True, vmem_limit_bytes=56 * 2**20),
    )(w, wo, x, g, wg, conv, rate, bias, gain)


def split_kernel(res_ref, sum_ref, out_ref, gin_ref, gates_ref, conv_ref, rate_ref, bias_ref, gain_ref):
    out_ref[...] = res_ref[0]
    gin_ref[...] = res_ref[1]
    heads = gates_ref.shape[1]
    count = gates_ref.shape[2] // 256
    for i in range(count):
        for j in range(2):
            for s in range(2):
                at = j * 4 + s * heads
                gates_ref[s, :, i * 256 + j * 128 : i * 256 + (j + 1) * 128] = sum_ref[i, at : at + heads, :]
    for s in range(3):
        for j in range(2):
            conv_ref[s, :, j * 128 : (j + 1) * 128] = sum_ref[count + s, j * 4 : j * 4 + 4, :]
    rest = sum_ref[count + 3]
    row = lax.broadcasted_iota(jnp.int32, rest.shape, 0)
    lane = lax.broadcasted_iota(jnp.int32, rest.shape, 1)
    for h in range(heads):
        rate_ref[h] = jnp.sum(jnp.where((row == 1) & (lane == h), rest, 0.0))
        bias_ref[h] = jnp.sum(jnp.where((row == 2) & (lane == h), rest, 0.0))
    gain_ref[...] = rest[0:1, :]


def on_device(dp, tensor, inputs, w_qkv, w_gates, conv_weight, decay_rate, gate_bias, norm_gain, w_out, grad_out):
    part, model = inputs.shape[2], w_gates.shape[1]
    heads, width = decay_rate.shape[0], w_qkv.shape[2]
    res, total = layer(
        dp, tensor, w_qkv, w_out.T, inputs[0].T, grad_out[0].T, w_gates.transpose(0, 2, 1), conv_weight,
        decay_rate, gate_bias, norm_gain[None],
    )
    vmem = pl.BlockSpec(memory_space=pltpu.VMEM)
    smem = pl.BlockSpec(memory_space=pltpu.SMEM)
    out, grad_in, gates, conv, rate, bias, gain = pl.pallas_call(
        split_kernel,
        name="split",
        out_shape=(
            jax.ShapeDtypeStruct((part, LEN), BF16),
            jax.ShapeDtypeStruct((part, LEN), BF16),
            jax.ShapeDtypeStruct((2, heads, model), F32),
            jax.ShapeDtypeStruct((3, TAPS, width), F32),
            jax.ShapeDtypeStruct((heads,), F32),
            jax.ShapeDtypeStruct((heads,), F32),
            jax.ShapeDtypeStruct((1, HEAD), F32),
        ),
        in_specs=[vmem] * 2,
        out_specs=(vmem,) * 4 + (smem,) * 2 + (vmem,),
    )(res, total)
    return (out.T[None], grad_in.T[None], gates.transpose(0, 2, 1), conv, rate, bias, gain[0])


def solution(mesh):
    dp, tensor = mesh.shape["dp"], mesh.shape["tensor"]
    return jax.shard_map(
        functools.partial(on_device, dp, tensor),
        mesh=mesh,
        in_specs=(
            P("dp", None, "tensor"),
            P(None, "dp", "tensor"),
            P(None, None, "tensor"),
            P(None, None, "tensor"),
            P("tensor"),
            P("tensor"),
            P(),
            P("tensor", "dp"),
            P("dp", None, "tensor"),
        ),
        out_specs=(
            P("dp", None, "tensor"),
            P("dp", None, "tensor"),
            P(None, None, "tensor"),
            P(None, None, "tensor"),
            P("tensor"),
            P("tensor"),
            P(),
        ),
        check_vma=False,
    )
```

```python
import functools
import math

import jax
import jax.numpy as jnp
from jax import lax
from jax.experimental import pallas as pl
from jax.experimental.pallas import tpu as pltpu
from jax.sharding import PartitionSpec as P

MESH = pl.DeviceIdType.MESH
F32, BF16 = jnp.float32, jnp.bfloat16
LEN = 128
HEAD = 128
TAPS = 4
CORES = 2
ZL = 2
EARLY = 2
NN = (((1,), (0,)), ((), ()))
NT = (((1,), (1,)), ((), ()))


class Place:
    def __init__(self, dp, tensor):
        self.ny = dp // (ZL * CORES)
        self.nz = 4 if tensor == 16 else 2
        self.nx = tensor // self.nz
        d, t = lax.axis_index("dp"), lax.axis_index("tensor")
        self.d, self.t = d, t
        self.zl = d // (self.ny * CORES)
        self.y = (d // CORES) % self.ny
        self.c = d % CORES
        self.zh = t // self.nx
        self.x = t % self.nx

    def dp_of(self, zl, y, c):
        return zl * (self.ny * CORES) + y * CORES + c

    def at_y(self, step):
        return self.dp_of(self.zl, (self.y + step + self.ny) % self.ny, self.c), self.t

    def at_z(self):
        return self.dp_of(1 - self.zl, self.y, self.c), self.t

    def at_core(self):
        return self.dp_of(self.zl, self.y, 1 - self.c), self.t

    def at_zh(self, step):
        return self.d, ((self.zh + step + self.nz) % self.nz) * self.nx + self.x

    def at_x(self, step):
        return self.d, self.zh * self.nx + (self.x + step + self.nx) % self.nx


def remote(src, dst, send, recv, where):
    return pltpu.make_async_remote_copy(
        src_ref=src, dst_ref=dst, send_sem=send, recv_sem=recv, device_id=where, device_id_type=MESH
    )


def meet(peers):
    barrier = pltpu.get_barrier_semaphore()
    for where in peers:
        pl.semaphore_signal(barrier, inc=1, device_id=where, device_id_type=MESH)
    pl.semaphore_wait(barrier, len(peers))


def halves(a):
    high = a.astype(BF16)
    return high, (a - high.astype(F32)).astype(BF16)


def dot(a, b, dims=NN):
    return lax.dot_general(a, b, dims, preferred_element_type=F32)


def product(a, b, dims=NN):
    ah, al = halves(a)
    bh, bl = halves(b)
    side = 0 if dims is NN else 1
    return dot(jnp.concatenate([ah, ah, al], 1), jnp.concatenate([bh, bl, bh], side), dims)


def triangle_product(triangle, a):
    high = a.astype(BF16)
    rest = a - high.astype(F32)
    mid = rest.astype(BF16)
    low = (rest - mid.astype(F32)).astype(BF16)
    return dot(jnp.concatenate([triangle] * 3, 1), jnp.concatenate([high, mid, low], 0))


def unit_inverse(lower, xor):
    inverse = jnp.where(xor == 0, 1.0, 0.0) - jnp.where(xor == 1, lower, 0.0)
    width = 2
    while width < lower.shape[0]:
        between = jnp.where((xor >= width) & (xor < 2 * width), lower, 0.0)
        inverse = inverse - product(product(inverse, between), inverse)
        width *= 2
    return inverse


def head_forward(q, k, v, beta, c_col, c_row, within, strict, xor):
    fading = jnp.where(within, jnp.exp(jnp.where(within, c_col - c_row, 0.0)), 0.0)
    faded_keys = jnp.where(strict, fading * product(k, k, NT), 0.0)
    lower = beta * faded_keys
    inverse = unit_inverse(lower, xor)
    rows = product(inverse, beta * v)
    scores = fading * product(q, k, NT)
    return fading, faded_keys, lower, inverse, rows, scores, product(scores, rows)


def head_backward(q, k, v, beta, fading, faded_keys, lower, inverse, rows, scores, d_out, within, strict):
    d_scores = jnp.where(within, product(d_out, rows, NT), 0.0)
    d_rows = product(scores.T, d_out)
    d_target = product(inverse.T, d_rows)
    d_lower = jnp.where(strict, -product(d_target, rows, NT), 0.0)
    faded = fading * d_scores
    both = beta * fading * d_lower
    dq = product(faded, k)
    dk = product(faded.T, q) + product(both + both.T, k)
    dv = beta * d_target
    spread = d_scores * scores + d_lower * lower
    dc = jnp.sum(spread - spread.T, 1, keepdims=True)
    d_beta = jnp.sum(d_lower * faded_keys + d_target * v, 1, keepdims=True)
    return dq, dk, dv, dc, d_beta


def shifted(a, step, row):
    if step == 0:
        return a
    size = a.shape[0]
    moved = pltpu.roll(a, step % size, 0)
    keep = row >= step if step > 0 else row < size + step
    return jnp.where(keep, moved, 0.0)


class Stream:
    def __init__(self, here, early, full, shard, sems):
        self.here, self.early, self.full = here, early, full
        self.far = here.ny // 2
        self.shard, self.half = shard, shard // 2
        self.yp, self.ym, self.z, self.c = (sems[i : i + 2] for i in (0, 2, 4, 6))
        self.sent = []

    def block(self, p, place, h, other_core=False):
        here = self.here
        zl = here.zl if p == 0 else 1 - here.zl
        c = 1 - here.c if other_core else here.c
        d = here.dp_of(zl, (here.y - place + here.ny) % here.ny, c)
        return self.full.at[:, pl.ds(pl.multiple_of(d * self.shard + h * self.half, 16), self.half), :]

    def send(self, ref, sems, index, where):
        copy = remote(ref, ref, sems[0].at[index], sems[1].at[index], where)
        copy.start()
        self.sent.append(copy)

    def arrive(self, ref, sems, index):
        remote(ref, ref, sems[0].at[index], sems[1].at[index], self.here.at_core()).wait_recv()

    def travels(self, direction, k, h):
        return k < self.far or (k == self.far and h == (0 if direction > 0 else 1))

    def along_y(self, ref, direction, k, p, h):
        if self.travels(direction, k, h):
            self.send(ref, self.yp if direction > 0 else self.ym, (k - 1, p, h), self.here.at_y(direction))

    def along_z(self, ref, place, h):
        self.send(ref, self.z, (place, h), self.here.at_z())

    def to_core(self, ref, p, place, h):
        self.send(ref, self.c, (p, place, h), self.here.at_core())

    def start(self):
        for h in range(2):
            own = self.block(0, 0, h)
            self.along_y(own, 1, 1, 0, h)
            self.along_y(own, -1, 1, 0, h)
            self.along_z(own, 0, h)

    def own_to_core(self):
        for h in range(2):
            self.to_core(self.block(0, 0, h), 0, 0, h)

    def places(self, k):
        return [k] if k in (0, self.far) else [k, self.here.ny - k]

    def from_z(self, k):
        if self.early and k:
            return
        for place in self.places(k):
            for h in range(2):
                got = self.block(1, place, h)
                self.arrive(got, self.z, (place, h))
                if self.early:
                    self.along_y(got, 1, 1, 1, h)
                    self.along_y(got, -1, 1, 1, h)
                self.to_core(got, 1, place, h)

    def from_y(self, k):
        for p in range(2 if self.early else 1):
            for h in range(2):
                for direction in (1, -1):
                    if not self.travels(direction, k, h):
                        continue
                    place = k if direction > 0 else self.here.ny - k
                    got = self.block(p, place, h)
                    self.arrive(got, self.yp if direction > 0 else self.ym, (k - 1, p, h))
                    self.along_y(got, direction, k + 1, p, h)
                    if not self.early:
                        self.along_z(got, place, h)
                    self.to_core(got, p, place, h)

    def from_core(self, k):
        for p in range(2):
            for place in self.places(k):
                for h in range(2):
                    self.arrive(self.block(p, place, h, True), self.c, (p, place, h))

    def finish(self):
        for copy in self.sent:
            copy.wait_send()


def stream_sems(ny, early):
    dma = pltpu.SemaphoreType.DMA
    sems = []
    for dims in ((ny // 2, 2 if early else 1, 2),) * 2 + ((1 if early else ny, 2), (2, ny, 2)):
        sems += [dma(dims), dma(dims)]
    return sems


def layer_kernel(
    dp, tensor, w_ref, wo_ref, x_ref, g_ref, wg_ref, conv_ref, rate_ref, bias_ref, gain_ref, res_ref, sum_ref, *scratch
):
    scratch = list(scratch)

    def take(n):
        out = scratch[:n]
        del scratch[:n]
        return out

    wf, xt, gt, xr, gr, wg16, gcol, proj, back, core_low, low, pack = take(12)
    parts, r1, relay, keep, r2, gx, gz, mine, ry, rz, fin, all_sums = take(12)
    own_sem, t1s, t1r, t2s, t2r, s0s, s0r, s1s, s1r, s2s, s2r, gxs, gxr, gzs, gzr, rys, ryr, rzs, rzr, ays, ayr = take(21)
    here = Place(dp, tensor)
    ny, nz, nx = here.ny, here.nz, here.nx
    far = ny // 2
    part = x_ref.shape[0]
    width = w_ref.shape[2]
    heads = width // HEAD
    each = pack.shape[0] // ny
    gate_tiles = xt.shape[0] // 256
    q = here.zl * CORES + here.c

    shard = w_ref.shape[1]
    early = Stream(here, True, wf.at[pl.ds(0, EARLY)], shard, take(8))
    late = Stream(here, False, wf.at[pl.ds(EARLY, 4 - EARLY)], shard, take(8))
    sent = []

    def at_q(r):
        other = q ^ r
        return here.dp_of(other // CORES, here.y, other % CORES), here.t

    def send(src, dst, s, r, where):
        copy = remote(src, dst, s, r, where)
        copy.start()
        sent.append(copy)

    def arrive(dst, s, r):
        remote(dst, dst, s, r, here.at_core()).wait_recv()

    def back_of(step, size, now):
        return (now - step + size) % size

    def slot(ref, t):
        return ref.at[pl.ds(pl.multiple_of(t * part, 16), part), :]

    mine_rows = pl.ds(pl.multiple_of(here.d * shard, 16), shard)
    own = [
        pltpu.make_async_copy(w_ref, wf.at[pl.ds(0, 3), mine_rows, :], own_sem.at[0]),
        pltpu.make_async_copy(wo_ref, wf.at[3, mine_rows, :], own_sem.at[1]),
        pltpu.make_async_copy(x_ref, slot(xt, here.t), own_sem.at[2]),
        pltpu.make_async_copy(g_ref, slot(gt, here.t), own_sem.at[3]),
    ]
    for copy in own:
        copy.start()
    meet(
        [here.at_y(s) for s in range(1, ny)]
        + [at_q(r) for r in range(1, 4)]
        + [here.at_zh(s) for s in range(1, nz)]
        + [here.at_x(s) for s in range(1, nx)]
    )

    arrays = (xt, gt)

    def set_out(a):
        got = slot(arrays[a], here.t)
        for s in sorted({1, nz - 1}):
            send(got, got, t1s.at[s - 1, a], t1r.at[s - 1, a], here.at_zh(s))
        for s in range(1, nx):
            send(got, got, t2s.at[s - 1, 0, a], t2r.at[s - 1, 0, a], here.at_x(s))

    for copy in own:
        copy.wait()
    late.start()
    early.start()
    set_out(0)
    late.own_to_core()
    early.own_to_core()
    early.from_z(0)

    proj[...] = jnp.zeros_like(proj)
    back[...] = jnp.zeros_like(back)
    pack[...] = jnp.zeros_like(pack)
    wide = wg_ref[...].astype(F32)
    wg16[...] = jnp.concatenate([wide[0], wide[1], jnp.zeros((16 - 2 * heads, wide.shape[2]), F32)], 0).astype(BF16)

    def column(i, _):
        at = pl.ds(pl.multiple_of(i * 128, 128), 128)
        tall = jnp.concatenate([wg16[:, at].astype(F32), jnp.zeros((112, 128), F32)], 0)
        gcol[at, :] = tall.T.astype(BF16)
        return 0

    lax.fori_loop(0, xt.shape[0] // 128, column, 0)

    def spread(a, steps):
        for s in steps:
            got = slot(arrays[a], back_of(s, nz, here.zh) * nx + here.x)
            arrive(got, t1s.at[s - 1, a], t1r.at[s - 1, a])
            if nz == 4 and s == (1 if a == 0 else 3):
                send(got, got, t1s.at[1, a], t1r.at[1, a], here.at_zh(1 if a == 0 else -1))
            for sx in range(1, nx):
                send(got, got, t2s.at[sx - 1, s, a], t2r.at[sx - 1, s, a], here.at_x(sx))

    near, further = sorted({1, nz - 1}), [2] if nz == 4 else []

    def landed(a, turned):
        dst = arrays[a]
        for s in range(nz):
            for sx in range(1, nx):
                got = slot(dst, back_of(s, nz, here.zh) * nx + back_of(sx, nx, here.x))
                arrive(got, t2s.at[sx - 1, s, a], t2r.at[sx - 1, s, a])

        def turn(t, _):
            turned[t] = dst[pl.ds(pl.multiple_of(t * part, 16), part), :].T
            return 0

        lax.fori_loop(0, tensor, turn, 0)

    def contract(k):
        early.from_core(k)
        late.from_core(k)
        ways = len(early.places(k))

        def term(i, _):
            zl = jnp.where(i // ways == 0, here.zl, 1 - here.zl)
            step = jnp.where(i % ways == 0, k, ny - k)
            t = zl * ny + (here.y - step + ny) % ny
            rows = pl.ds(pl.multiple_of(t * part, 16), part)
            x = xr[t]
            for s in range(3):
                proj[:, s * width : (s + 1) * width] += dot(x, wf[s, rows, :])
            return 0

        lax.fori_loop(0, 2 * ways, term, 0)

    for k in range(1, far + 1):
        deep = k == far and far > 2
        if deep:
            landed(0, xr)
            for j in range(far - 1):
                contract(j)
        late.from_y(k)
        if deep:
            late.from_z(k - 1)
            landed(1, gr)
            logits_t = dot(wg16[...], xt[...])
        early.from_y(k)
        if not deep:
            late.from_z(k - 1)
        if k == 1:
            spread(0, near)
            set_out(1)
        if k == min(2, far):
            spread(0, further)
            spread(1, near)
        if k == min(3, far):
            spread(1, further)
    late.from_z(far)
    if far <= 2:
        landed(0, xr)
        landed(1, gr)
        logits_t = dot(wg16[...], xt[...])
        for j in range(far - 1):
            contract(j)
    contract(far - 1)
    contract(far)

    row = lax.broadcasted_iota(jnp.int32, (LEN, LEN), 0)
    lane = lax.broadcasted_iota(jnp.int32, (LEN, LEN), 1)
    wide_row = lax.broadcasted_iota(jnp.int32, (LEN, width), 0)
    within, strict, xor = row >= lane, row > lane, row ^ lane
    triangle = jnp.where(within, 1.0, 0.0).astype(BF16)
    triangle_t = jnp.where(row <= lane, 1.0, 0.0).astype(BF16)
    lane_1 = lax.broadcasted_iota(jnp.int32, (1, LEN), 1)
    rate = sum(jnp.where(lane_1 == h, rate_ref[h], 0.0) for h in range(heads))
    bias = sum(jnp.where(lane_1 == h, bias_ref[h], 0.0) for h in range(heads))
    gain = gain_ref[...]

    logits = jnp.concatenate([logits_t, jnp.zeros((LEN - 16, LEN), F32)], 0).T
    pre = logits + bias
    soft = jnp.maximum(pre, 0.0) + jnp.log1p(jnp.exp(-jnp.abs(pre)))
    strength = 1.0 / (1.0 + jnp.exp(-logits))
    cumulative = triangle_product(triangle, -rate * soft)
    cumulative_t = cumulative.T

    before, gate, active = [], [], []
    for s in range(3):
        p = proj[:, s * width : (s + 1) * width]
        z = jnp.zeros_like(p)
        for i in range(TAPS):
            z = z + conv_ref[s, i : i + 1, :] * shifted(p, TAPS - 1 - i, wide_row)
        sigma = 1.0 / (1.0 + jnp.exp(-z))
        before.append(z)
        gate.append(sigma)
        active.append(z * sigma)

    scale = 1.0 / math.sqrt(HEAD)
    kept = []
    for h in range(heads):
        cut = slice(h * HEAD, (h + 1) * HEAD)
        aq, ak, v = active[0][:, cut], active[1][:, cut], active[2][:, cut]
        nq = lax.rsqrt(jnp.sum(aq * aq, 1, keepdims=True) + 1e-6)
        nk = lax.rsqrt(jnp.sum(ak * ak, 1, keepdims=True) + 1e-6)
        uq, k = aq * nq, ak * nk
        beta = strength[:, heads + h : heads + h + 1]
        held = head_forward(uq * scale, k, v, beta, cumulative[:, h : h + 1], cumulative_t[h : h + 1, :], within, strict, xor)
        out = held[-1]
        r = lax.rsqrt(jnp.mean(out * out, 1, keepdims=True) + 1e-5)
        normed = out * r
        core_low[:, cut] = (normed * gain).astype(BF16)
        kept.append((nq, nk, uq, k, v, beta, held[:-1], r, normed))

    part_half = part // 2
    ends = [slice(0, part_half), slice(part_half, part)]
    opposite = nx == 4
    ways = [1, -1] if opposite else [1]

    def along_x(a, sz, t, side, h):
        rows = pl.ds(h * part_half, part_half)
        return remote(
            parts.at[a, t, rows], r1.at[a, side, sz, rows], s1s.at[a, side, sz, h], s1r.at[a, side, sz, h], here.at_x(ways[side])
        )

    def across(a, sz, t, h):
        rows = pl.ds(h * part_half, part_half)
        return remote(parts.at[a, t, rows], relay.at[a, sz, h], s0s.at[a, sz, h], s0r.at[a, sz, h], here.at_x(ways[h]))

    def owner(sz, sx):
        return ((here.zh + sz) % nz) * nx + (here.x + sx + nx) % nx

    def pass_on(a, sz):
        for h, way in enumerate(ways if opposite else []):
            t = owner(sz, way)
            across(a, sz, t, h).wait_recv()
            parts[a, t, ends[h], :] = (parts[a, t, ends[h], :].astype(F32) + relay[a, sz, h].astype(F32)).astype(BF16)
            along_x(a, sz, t, h, h).start()

    def make(a, sz, build):
        for sx in [2, *ways, 0] if opposite else [*ways, 0]:
            t = owner(sz, sx)
            parts[a, t] = build(pl.ds(pl.multiple_of(t * part, 16), part)).astype(BF16)

    def ship(a, sz):
        if opposite:
            for h in range(2):
                across(a, sz, owner(sz, 2), h).start()
        for side, way in enumerate(ways):
            for h in range(2):
                if not opposite or h != side:
                    along_x(a, sz, owner(sz, way), side, h).start()

    def each_away(body):
        def step(sz, _):
            body(sz)
            return 0

        lax.fori_loop(1, nz, step, 0)

    def second(a, steps):
        for sz in steps:
            total = parts[a, owner(sz, 0)].astype(F32)
            for side in range(len(ways)):
                for h in range(2):
                    along_x(a, sz, 0, side, h).wait_recv()
                total = total + r1[a, side, sz].astype(F32)
            if sz:
                mine[a, sz] = total.astype(BF16)
                send(mine.at[a, sz], r2.at[a, sz], s2s.at[a, sz], s2r.at[a, sz], here.at_zh(sz))
            else:
                keep[a] = total

    def last(a):
        total = keep[a]
        for sz in range(1, nz):
            arrive(r2.at[a, sz], s2s.at[a, sz], s2r.at[a, sz])
            total = total + r2[a, sz].astype(F32)
        res_ref[a] = total.astype(BF16)

    def out_part(rows):
        return dot(wf[3, rows, :], core_low[...], NT)

    def out_step(sz):
        make(0, sz, out_part)
        ship(0, sz)

    each_away(out_step)

    def back_term(t, _):
        back[...] += dot(gr[t], wf[3, pl.ds(pl.multiple_of(t * part, 16), part), :])
        return 0

    lax.fori_loop(0, tensor, back_term, 0)
    make(0, 0, out_part)
    each_away(lambda sz: pass_on(0, sz))

    gain_grad = jnp.zeros((1, HEAD), F32)
    for h in range(heads):
        gain_grad = gain_grad + jnp.sum(back[:, h * HEAD : (h + 1) * HEAD] * kept[h][-1], 0, keepdims=True)
    gx[here.x] = jnp.concatenate([gain_grad, jnp.zeros((7, HEAD), F32)], 0)
    for s in range(1, nx):
        send(gx.at[here.x], gx.at[here.x], gxs.at[s - 1], gxr.at[s - 1], here.at_x(s))

    d_active = [[None] * heads for _ in range(3)]
    dc_all = jnp.zeros((LEN, LEN), F32)
    db_all = jnp.zeros((LEN, LEN), F32)
    for h in range(heads):
        nq, nk, uq, k, v, beta, held, r, normed = kept[h]
        dn = back[:, h * HEAD : (h + 1) * HEAD] * gain
        d_out = r * (dn - normed * jnp.mean(dn * normed, 1, keepdims=True))
        dq, dk, dv, dc, d_beta = head_backward(uq * scale, k, v, beta, *held, d_out, within, strict)
        dq = dq * scale
        d_active[0][h] = nq * (dq - uq * jnp.sum(uq * dq, 1, keepdims=True))
        d_active[1][h] = nk * (dk - k * jnp.sum(k * dk, 1, keepdims=True))
        d_active[2][h] = dv
        dc_all = jnp.where(lane == h, dc, dc_all)
        db_all = jnp.where(lane == heads + h, d_beta, db_all)

    for s in range(1, nx):
        arrive(gx.at[back_of(s, nx, here.x)], gxs.at[s - 1], gxr.at[s - 1])
    gz[here.zh] = sum(gx[i] for i in range(nx))
    for s in range(1, nz):
        send(gz.at[here.zh], gz.at[here.zh], gzs.at[s - 1], gzr.at[s - 1], here.at_zh(s))

    d_decay = triangle_product(triangle_t, dc_all)
    d_pre = -rate * d_decay / (1.0 + jnp.exp(-pre))
    pack[gate_tiles + 3, 1:2, :] = jnp.sum(-soft * d_decay, 0, keepdims=True)
    pack[gate_tiles + 3, 2:3, :] = jnp.sum(d_pre, 0, keepdims=True)
    d_logits = (d_pre + db_all * strength * (1.0 - strength)).astype(BF16)
    low[:, 3 * width :] = d_logits
    d_logits_t = d_logits.astype(F32).T[0:16, :].astype(BF16)

    for s in range(3):
        z, sigma = before[s], gate[s]
        dz = jnp.concatenate(d_active[s], 1) * (sigma * (1.0 + z * (1.0 - sigma)))
        p = proj[:, s * width : (s + 1) * width]
        dp_s = jnp.zeros_like(p)
        for i in range(TAPS):
            ahead = shifted(dz, i + 1 - TAPS, wide_row)
            dp_s = dp_s + conv_ref[s, i : i + 1, :] * ahead
            total = jnp.sum(ahead * p, 0, keepdims=True)
            for j in range(width // 128):
                at = j * TAPS + i
                pack[gate_tiles + s, at : at + 1, :] = total[:, j * 128 : (j + 1) * 128]
        low[:, s * width : (s + 1) * width] = dp_s.astype(BF16)

    def grad_in(rows):
        total = dot(gcol[rows, :], low[:, 3 * width :], NT)
        for s in range(3):
            total = total + dot(wf[s, rows, :], low[:, s * width : (s + 1) * width], NT)
        return total

    def grad_step(sz):
        make(1, sz, grad_in)
        ship(1, sz)

    each_away(grad_step)
    make(1, 0, grad_in)

    def gates(i, _):
        grad = dot(d_logits_t, xt[pl.ds(pl.multiple_of(i * 256, 256), 256), :], NT)
        pack[i, 0:4, :] = grad[0:4, 0:128]
        pack[i, 4:8, :] = grad[0:4, 128:256]
        return 0

    lax.fori_loop(0, gate_tiles, gates, 0)

    for s in range(1, nz):
        arrive(gz.at[back_of(s, nz, here.zh)], gzs.at[s - 1], gzr.at[s - 1])
    pack[gate_tiles + 3, 0:1, :] = sum(gz[i, 0:1, :] for i in range(nz))
    for s in range(1, ny):
        there = (here.y + s) % ny
        send(pack.at[pl.ds(there * each, each)], ry.at[here.y], rys.at[s - 1], ryr.at[s - 1], here.at_y(s))
    ry[here.y] = pack[pl.ds(here.y * each, each)]

    away = range(1, nz)
    second(0, away)
    each_away(lambda sz: pass_on(1, sz))
    ship(1, 0)
    ship(0, 0)

    for s in range(1, ny):
        arrive(ry.at[back_of(s, ny, here.y)], rys.at[s - 1], ryr.at[s - 1])
    rz[q] = sum(ry[i] for i in range(ny))
    for r in range(1, 4):
        send(rz.at[q], rz.at[q], rzs.at[r - 1], rzr.at[r - 1], at_q(r))

    second(1, away)
    pass_on(1, 0)
    pass_on(0, 0)

    for r in range(1, 4):
        arrive(rz.at[q ^ r], rzs.at[r - 1], rzr.at[r - 1])
    fin[...] = sum(rz[i] for i in range(4))
    for s in range(1, ny):
        send(fin, all_sums.at[here.y], ays.at[s - 1], ayr.at[s - 1], here.at_y(s))
    all_sums[here.y] = fin[...]

    second(1, [0])
    second(0, [0])
    last(0)

    for s in range(1, ny):
        arrive(all_sums.at[back_of(s, ny, here.y)], ays.at[s - 1], ayr.at[s - 1])
    for i in range(ny):
        sum_ref[i * each : (i + 1) * each] = all_sums[i]

    last(1)

    def finished(sz, _):
        for a in range(2):
            for h in range(2):
                for side in range(len(ways)):
                    along_x(a, sz, 0, side, h).wait_send()
                if opposite:
                    across(a, sz, 0, h).wait_send()
        return 0

    lax.fori_loop(0, nz, finished, 0)
    early.finish()
    late.finish()
    for copy in sent:
        copy.wait_send()


def layer(dp, tensor, w, wo, x, g, wg, conv, rate, bias, gain):
    ny = dp // (ZL * CORES)
    nz = 4 if tensor == 16 else 2
    nx = tensor // nz
    part = x.shape[0]
    model, width = part * tensor, w.shape[2]
    tiles = pl.cdiv(model // 256 + 4, ny) * ny
    each = tiles // ny
    any_spec = pl.BlockSpec(memory_space=pl.ANY)
    vmem = pl.BlockSpec(memory_space=pltpu.VMEM)
    smem = pl.BlockSpec(memory_space=pltpu.SMEM)
    dma = pltpu.SemaphoreType.DMA
    sems = [dma((4,))]
    for dims in (
        (nz - 1, 2), (nx - 1, nz, 2), (2, nz, 2), (2, 2, nz, 2), (2, nz), (nx - 1,), (nz - 1,), (ny - 1,), (3,), (ny - 1,),
    ):
        sems += [dma(dims), dma(dims)]
    sems += stream_sems(ny, True) + stream_sems(ny, False)
    return pl.pallas_call(
        functools.partial(layer_kernel, dp, tensor),
        name="layer",
        out_shape=(jax.ShapeDtypeStruct((2, part, LEN), BF16), jax.ShapeDtypeStruct((tiles, 8, 128), F32)),
        in_specs=[any_spec] * 4 + [vmem] * 2 + [smem] * 2 + [vmem],
        out_specs=(vmem,) * 2,
        scratch_shapes=[
            pltpu.VMEM((4, model, width), BF16),
            pltpu.VMEM((model, LEN), BF16),
            pltpu.VMEM((model, LEN), BF16),
            pltpu.VMEM((tensor, LEN, part), BF16),
            pltpu.VMEM((tensor, LEN, part), BF16),
            pltpu.VMEM((16, model), BF16),
            pltpu.VMEM((model, 128), BF16),
            pltpu.VMEM((LEN, 3 * width), F32),
            pltpu.VMEM((LEN, width), F32),
            pltpu.VMEM((LEN, width), BF16),
            pltpu.VMEM((LEN, 3 * width + 128), BF16),
            pltpu.VMEM((tiles, 8, 128), F32),
            pltpu.VMEM((2, tensor, part, LEN), BF16),
            pltpu.VMEM((2, 2, nz, part, LEN), BF16),
            pltpu.VMEM((2, nz, 2, part // 2, LEN), BF16),
            pltpu.VMEM((2, part, LEN), F32),
            pltpu.VMEM((2, nz, part, LEN), BF16),
            pltpu.VMEM((nx, 8, 128), F32),
            pltpu.VMEM((nz, 8, 128), F32),
            pltpu.VMEM((2, nz, part, LEN), BF16),
            pltpu.VMEM((ny, each, 8, 128), F32),
            pltpu.VMEM((4, each, 8, 128), F32),
            pltpu.VMEM((each, 8, 128), F32),
            pltpu.VMEM((ny, each, 8, 128), F32),
        ]
        + sems,
        compiler_params=pltpu.CompilerParams(collective_id=0, has_side_effects=True, vmem_limit_bytes=56 * 2**20),
    )(w, wo, x, g, wg, conv, rate, bias, gain)


def split_kernel(res_ref, sum_ref, out_ref, gin_ref, gates_ref, conv_ref, rate_ref, bias_ref, gain_ref):
    out_ref[...] = res_ref[0]
    gin_ref[...] = res_ref[1]
    heads = gates_ref.shape[1]
    count = gates_ref.shape[2] // 256
    for i in range(count):
        for j in range(2):
            for s in range(2):
                at = j * 4 + s * heads
                gates_ref[s, :, i * 256 + j * 128 : i * 256 + (j + 1) * 128] = sum_ref[i, at : at + heads, :]
    for s in range(3):
        for j in range(2):
            conv_ref[s, :, j * 128 : (j + 1) * 128] = sum_ref[count + s, j * 4 : j * 4 + 4, :]
    rest = sum_ref[count + 3]
    row = lax.broadcasted_iota(jnp.int32, rest.shape, 0)
    lane = lax.broadcasted_iota(jnp.int32, rest.shape, 1)
    for h in range(heads):
        rate_ref[h] = jnp.sum(jnp.where((row == 1) & (lane == h), rest, 0.0))
        bias_ref[h] = jnp.sum(jnp.where((row == 2) & (lane == h), rest, 0.0))
    gain_ref[...] = rest[0:1, :]


def on_device(dp, tensor, inputs, w_qkv, w_gates, conv_weight, decay_rate, gate_bias, norm_gain, w_out, grad_out):
    part, model = inputs.shape[2], w_gates.shape[1]
    heads, width = decay_rate.shape[0], w_qkv.shape[2]
    res, total = layer(
        dp, tensor, w_qkv, w_out.T, inputs[0].T, grad_out[0].T, w_gates.transpose(0, 2, 1), conv_weight,
        decay_rate, gate_bias, norm_gain[None],
    )
    vmem = pl.BlockSpec(memory_space=pltpu.VMEM)
    smem = pl.BlockSpec(memory_space=pltpu.SMEM)
    out, grad_in, gates, conv, rate, bias, gain = pl.pallas_call(
        split_kernel,
        name="split",
        out_shape=(
            jax.ShapeDtypeStruct((part, LEN), BF16),
            jax.ShapeDtypeStruct((part, LEN), BF16),
            jax.ShapeDtypeStruct((2, heads, model), F32),
            jax.ShapeDtypeStruct((3, TAPS, width), F32),
            jax.ShapeDtypeStruct((heads,), F32),
            jax.ShapeDtypeStruct((heads,), F32),
            jax.ShapeDtypeStruct((1, HEAD), F32),
        ),
        in_specs=[vmem] * 2,
        out_specs=(vmem,) * 4 + (smem,) * 2 + (vmem,),
    )(res, total)
    return (out.T[None], grad_in.T[None], gates.transpose(0, 2, 1), conv, rate, bias, gain[0])


def solution(mesh):
    dp, tensor = mesh.shape["dp"], mesh.shape["tensor"]
    return jax.shard_map(
        functools.partial(on_device, dp, tensor),
        mesh=mesh,
        in_specs=(
            P("dp", None, "tensor"),
            P(None, "dp", "tensor"),
            P(None, None, "tensor"),
            P(None, None, "tensor"),
            P("tensor"),
            P("tensor"),
            P(),
            P("tensor", "dp"),
            P("dp", None, "tensor"),
        ),
        out_specs=(
            P("dp", None, "tensor"),
            P("dp", None, "tensor"),
            P(None, None, "tensor"),
            P(None, None, "tensor"),
            P("tensor"),
            P("tensor"),
            P(),
        ),
        check_vma=False,
    )
```

```python
import functools
import math

import jax
import jax.numpy as jnp
from jax import lax
from jax.experimental import pallas as pl
from jax.experimental.pallas import tpu as pltpu
from jax.sharding import PartitionSpec as P

MESH = pl.DeviceIdType.MESH
F32, BF16 = jnp.float32, jnp.bfloat16
LEN = 128
HEAD = 128
TAPS = 4
CORES = 2
ZL = 2
EARLY = 2
NN = (((1,), (0,)), ((), ()))
NT = (((1,), (1,)), ((), ()))


class Place:
    def __init__(self, dp, tensor):
        self.ny = dp // (ZL * CORES)
        self.nz = 4 if tensor == 16 else 2
        self.nx = tensor // self.nz
        d, t = lax.axis_index("dp"), lax.axis_index("tensor")
        self.d, self.t = d, t
        self.zl = d // (self.ny * CORES)
        self.y = (d // CORES) % self.ny
        self.c = d % CORES
        self.zh = t // self.nx
        self.x = t % self.nx

    def dp_of(self, zl, y, c):
        return zl * (self.ny * CORES) + y * CORES + c

    def at_y(self, step):
        return self.dp_of(self.zl, (self.y + step + self.ny) % self.ny, self.c), self.t

    def at_z(self):
        return self.dp_of(1 - self.zl, self.y, self.c), self.t

    def at_core(self):
        return self.dp_of(self.zl, self.y, 1 - self.c), self.t

    def at_zh(self, step):
        return self.d, ((self.zh + step + self.nz) % self.nz) * self.nx + self.x

    def at_x(self, step):
        return self.d, self.zh * self.nx + (self.x + step + self.nx) % self.nx


def remote(src, dst, send, recv, where):
    return pltpu.make_async_remote_copy(
        src_ref=src, dst_ref=dst, send_sem=send, recv_sem=recv, device_id=where, device_id_type=MESH
    )


def meet(peers):
    barrier = pltpu.get_barrier_semaphore()
    for where in peers:
        pl.semaphore_signal(barrier, inc=1, device_id=where, device_id_type=MESH)
    pl.semaphore_wait(barrier, len(peers))


def halves(a):
    high = a.astype(BF16)
    return high, (a - high.astype(F32)).astype(BF16)


def dot(a, b, dims=NN):
    return lax.dot_general(a, b, dims, preferred_element_type=F32)


def product(a, b, dims=NN):
    ah, al = halves(a)
    bh, bl = halves(b)
    side = 0 if dims is NN else 1
    return dot(jnp.concatenate([ah, ah, al], 1), jnp.concatenate([bh, bl, bh], side), dims)


def triangle_product(triangle, a):
    high = a.astype(BF16)
    rest = a - high.astype(F32)
    mid = rest.astype(BF16)
    low = (rest - mid.astype(F32)).astype(BF16)
    return dot(jnp.concatenate([triangle] * 3, 1), jnp.concatenate([high, mid, low], 0))


def unit_inverse(lower, xor):
    inverse = jnp.where(xor == 0, 1.0, 0.0) - jnp.where(xor == 1, lower, 0.0)
    width = 2
    while width < lower.shape[0]:
        between = jnp.where((xor >= width) & (xor < 2 * width), lower, 0.0)
        inverse = inverse - product(product(inverse, between), inverse)
        width *= 2
    return inverse


def head_forward(q, k, v, beta, c_col, c_row, within, strict, xor):
    fading = jnp.where(within, jnp.exp(jnp.where(within, c_col - c_row, 0.0)), 0.0)
    faded_keys = jnp.where(strict, fading * product(k, k, NT), 0.0)
    lower = beta * faded_keys
    inverse = unit_inverse(lower, xor)
    rows = product(inverse, beta * v)
    scores = fading * product(q, k, NT)
    return fading, faded_keys, lower, inverse, rows, scores, product(scores, rows)


def head_backward(q, k, v, beta, fading, faded_keys, lower, inverse, rows, scores, d_out, within, strict):
    d_scores = jnp.where(within, product(d_out, rows, NT), 0.0)
    d_rows = product(scores.T, d_out)
    d_target = product(inverse.T, d_rows)
    d_lower = jnp.where(strict, -product(d_target, rows, NT), 0.0)
    faded = fading * d_scores
    both = beta * fading * d_lower
    dq = product(faded, k)
    dk = product(faded.T, q) + product(both + both.T, k)
    dv = beta * d_target
    spread = d_scores * scores + d_lower * lower
    dc = jnp.sum(spread - spread.T, 1, keepdims=True)
    d_beta = jnp.sum(d_lower * faded_keys + d_target * v, 1, keepdims=True)
    return dq, dk, dv, dc, d_beta


def shifted(a, step, row):
    if step == 0:
        return a
    size = a.shape[0]
    moved = pltpu.roll(a, step % size, 0)
    keep = row >= step if step > 0 else row < size + step
    return jnp.where(keep, moved, 0.0)


class Stream:
    def __init__(self, here, early, full, shard, sems):
        self.here, self.early, self.full = here, early, full
        self.far = here.ny // 2
        self.shard, self.half = shard, shard // 2
        self.yp, self.ym, self.z, self.c = (sems[i : i + 2] for i in (0, 2, 4, 6))
        self.sent = []

    def block(self, p, place, h, other_core=False):
        here = self.here
        zl = here.zl if p == 0 else 1 - here.zl
        c = 1 - here.c if other_core else here.c
        d = here.dp_of(zl, (here.y - place + here.ny) % here.ny, c)
        return self.full.at[:, pl.ds(pl.multiple_of(d * self.shard + h * self.half, 16), self.half), :]

    def send(self, ref, sems, index, where):
        copy = remote(ref, ref, sems[0].at[index], sems[1].at[index], where)
        copy.start()
        self.sent.append(copy)

    def arrive(self, ref, sems, index):
        remote(ref, ref, sems[0].at[index], sems[1].at[index], self.here.at_core()).wait_recv()

    def travels(self, direction, k, h):
        return k < self.far or (k == self.far and h == (0 if direction > 0 else 1))

    def along_y(self, ref, direction, k, p, h):
        if self.travels(direction, k, h):
            self.send(ref, self.yp if direction > 0 else self.ym, (k - 1, p, h), self.here.at_y(direction))

    def along_z(self, ref, place, h):
        self.send(ref, self.z, (place, h), self.here.at_z())

    def to_core(self, ref, p, place, h):
        self.send(ref, self.c, (p, place, h), self.here.at_core())

    def start(self):
        for h in range(2):
            own = self.block(0, 0, h)
            self.along_y(own, 1, 1, 0, h)
            self.along_y(own, -1, 1, 0, h)

    def own_to_z(self):
        for h in range(2):
            self.along_z(self.block(0, 0, h), 0, h)

    def own_to_core(self):
        for h in range(2):
            self.to_core(self.block(0, 0, h), 0, 0, h)

    def places(self, k):
        return [k] if k in (0, self.far) else [k, self.here.ny - k]

    def from_z(self, k):
        if self.early and k:
            return
        for place in self.places(k):
            for h in range(2):
                got = self.block(1, place, h)
                self.arrive(got, self.z, (place, h))
                if self.early:
                    self.along_y(got, 1, 1, 1, h)
                    self.along_y(got, -1, 1, 1, h)
                self.to_core(got, 1, place, h)

    def from_y(self, k):
        for p in range(2 if self.early else 1):
            for h in range(2):
                for direction in (1, -1):
                    if not self.travels(direction, k, h):
                        continue
                    place = k if direction > 0 else self.here.ny - k
                    got = self.block(p, place, h)
                    self.arrive(got, self.yp if direction > 0 else self.ym, (k - 1, p, h))
                    self.along_y(got, direction, k + 1, p, h)
                    if not self.early:
                        self.along_z(got, place, h)
                    self.to_core(got, p, place, h)

    def from_core(self, k):
        for p in range(2):
            for place in self.places(k):
                for h in range(2):
                    self.arrive(self.block(p, place, h, True), self.c, (p, place, h))

    def finish(self):
        for copy in self.sent:
            copy.wait_send()


def stream_sems(ny, early):
    dma = pltpu.SemaphoreType.DMA
    sems = []
    for dims in ((ny // 2, 2 if early else 1, 2),) * 2 + ((1 if early else ny, 2), (2, ny, 2)):
        sems += [dma(dims), dma(dims)]
    return sems


def layer_kernel(
    dp, tensor, w_ref, wo_ref, x_ref, g_ref, wg_ref, conv_ref, rate_ref, bias_ref, gain_ref, res_ref, sum_ref, *scratch
):
    scratch = list(scratch)

    def take(n):
        out = scratch[:n]
        del scratch[:n]
        return out

    wf, xt, gt, xr, gr, wg16, gcol, proj, back, core_low, low, pack = take(12)
    parts, r1, relay, keep, r2, gx, gz, mine, ry, rz, fin, all_sums = take(12)
    own_sem, t1s, t1r, t2s, t2r, s0s, s0r, s1s, s1r, s2s, s2r, gxs, gxr, gzs, gzr, rys, ryr, rzs, rzr, ays, ayr = take(21)
    here = Place(dp, tensor)
    ny, nz, nx = here.ny, here.nz, here.nx
    far = ny // 2
    part = x_ref.shape[0]
    width = w_ref.shape[2]
    heads = width // HEAD
    each = pack.shape[0] // ny
    gate_tiles = xt.shape[0] // 256
    q = here.zl * CORES + here.c

    shard = w_ref.shape[1]
    early = Stream(here, True, wf.at[pl.ds(0, EARLY)], shard, take(8))
    late = Stream(here, False, wf.at[pl.ds(EARLY, 4 - EARLY)], shard, take(8))
    sent = []

    def at_q(r):
        other = q ^ r
        return here.dp_of(other // CORES, here.y, other % CORES), here.t

    def send(src, dst, s, r, where):
        copy = remote(src, dst, s, r, where)
        copy.start()
        sent.append(copy)

    def arrive(dst, s, r):
        remote(dst, dst, s, r, here.at_core()).wait_recv()

    def back_of(step, size, now):
        return (now - step + size) % size

    def slot(ref, t):
        return ref.at[pl.ds(pl.multiple_of(t * part, 16), part), :]

    mine_rows = pl.ds(pl.multiple_of(here.d * shard, 16), shard)
    own = [
        pltpu.make_async_copy(w_ref, wf.at[pl.ds(0, 3), mine_rows, :], own_sem.at[0]),
        pltpu.make_async_copy(wo_ref, wf.at[3, mine_rows, :], own_sem.at[1]),
        pltpu.make_async_copy(x_ref, slot(xt, here.t), own_sem.at[2]),
        pltpu.make_async_copy(g_ref, slot(gt, here.t), own_sem.at[3]),
    ]
    for copy in own:
        copy.start()
    meet(
        [here.at_y(s) for s in range(1, ny)]
        + [at_q(r) for r in range(1, 4)]
        + [here.at_zh(s) for s in range(1, nz)]
        + [here.at_x(s) for s in range(1, nx)]
    )

    arrays = (xt, gt)

    def set_out(a):
        got = slot(arrays[a], here.t)
        for s in sorted({1, nz - 1}):
            send(got, got, t1s.at[s - 1, a], t1r.at[s - 1, a], here.at_zh(s))
        for s in range(1, nx):
            send(got, got, t2s.at[s - 1, 0, a], t2r.at[s - 1, 0, a], here.at_x(s))

    for copy in own:
        copy.wait()
    early.own_to_z()
    late.start()
    early.start()
    set_out(0)
    late.own_to_z()
    late.own_to_core()
    early.own_to_core()
    early.from_z(0)

    proj[...] = jnp.zeros_like(proj)
    back[...] = jnp.zeros_like(back)
    pack[...] = jnp.zeros_like(pack)
    wide = wg_ref[...].astype(F32)
    wg16[...] = jnp.concatenate([wide[0], wide[1], jnp.zeros((16 - 2 * heads, wide.shape[2]), F32)], 0).astype(BF16)

    def column(i, _):
        at = pl.ds(pl.multiple_of(i * 128, 128), 128)
        tall = jnp.concatenate([wg16[:, at].astype(F32), jnp.zeros((112, 128), F32)], 0)
        gcol[at, :] = tall.T.astype(BF16)
        return 0

    lax.fori_loop(0, xt.shape[0] // 128, column, 0)

    row = lax.broadcasted_iota(jnp.int32, (LEN, LEN), 0)
    lane = lax.broadcasted_iota(jnp.int32, (LEN, LEN), 1)
    wide_row = lax.broadcasted_iota(jnp.int32, (LEN, width), 0)
    within, strict, xor = row >= lane, row > lane, row ^ lane
    triangle = jnp.where(within, 1.0, 0.0).astype(BF16)
    triangle_t = jnp.where(row <= lane, 1.0, 0.0).astype(BF16)
    lane_1 = lax.broadcasted_iota(jnp.int32, (1, LEN), 1)
    rate = sum(jnp.where(lane_1 == h, rate_ref[h], 0.0) for h in range(heads))
    bias = sum(jnp.where(lane_1 == h, bias_ref[h], 0.0) for h in range(heads))
    gain = gain_ref[...]

    def spread(a, steps):
        for s in steps:
            got = slot(arrays[a], back_of(s, nz, here.zh) * nx + here.x)
            arrive(got, t1s.at[s - 1, a], t1r.at[s - 1, a])
            if nz == 4 and s == (1 if a == 0 else 3):
                send(got, got, t1s.at[1, a], t1r.at[1, a], here.at_zh(1 if a == 0 else -1))
            for sx in range(1, nx):
                send(got, got, t2s.at[sx - 1, s, a], t2r.at[sx - 1, s, a], here.at_x(sx))

    near, further = sorted({1, nz - 1}), [2] if nz == 4 else []

    def landed(a, turned):
        dst = arrays[a]
        for s in range(nz):
            for sx in range(1, nx):
                got = slot(dst, back_of(s, nz, here.zh) * nx + back_of(sx, nx, here.x))
                arrive(got, t2s.at[sx - 1, s, a], t2r.at[sx - 1, s, a])

        def turn(t, _):
            turned[t] = dst[pl.ds(pl.multiple_of(t * part, 16), part), :].T
            return 0

        lax.fori_loop(0, tensor, turn, 0)

    def decays():
        logits_t = dot(wg16[...], xt[...])
        logits = jnp.concatenate([logits_t, jnp.zeros((LEN - 16, LEN), F32)], 0).T
        pre = logits + bias
        soft = jnp.maximum(pre, 0.0) + jnp.log1p(jnp.exp(-jnp.abs(pre)))
        strength = 1.0 / (1.0 + jnp.exp(-logits))
        cumulative = triangle_product(triangle, -rate * soft)
        cumulative_t = cumulative.T
        return logits, pre, soft, strength, cumulative, cumulative_t

    def contract(k):
        early.from_core(k)
        late.from_core(k)
        ways = len(early.places(k))

        def term(i, _):
            zl = jnp.where(i // ways == 0, here.zl, 1 - here.zl)
            step = jnp.where(i % ways == 0, k, ny - k)
            t = zl * ny + (here.y - step + ny) % ny
            rows = pl.ds(pl.multiple_of(t * part, 16), part)
            x = xr[t]
            for s in range(3):
                proj[:, s * width : (s + 1) * width] += dot(x, wf[s, rows, :])
            return 0

        lax.fori_loop(0, 2 * ways, term, 0)

    for k in range(1, far + 1):
        deep = k == far and far > 2
        if deep:
            landed(0, xr)
            for j in range(far - 1):
                contract(j)
        late.from_y(k)
        if deep:
            late.from_z(k - 1)
            landed(1, gr)
            contract(k - 1)
            logits, pre, soft, strength, cumulative, cumulative_t = decays()
        early.from_y(k)
        if not deep:
            late.from_z(k - 1)
        if k == 1:
            spread(0, near)
            set_out(1)
        if k == min(2, far):
            spread(0, further)
            spread(1, near)
        if k == min(3, far):
            spread(1, further)
    late.from_z(far)
    if far <= 2:
        landed(0, xr)
        landed(1, gr)
        logits, pre, soft, strength, cumulative, cumulative_t = decays()
        for j in range(far):
            contract(j)
    contract(far)

    before, gate, active = [], [], []
    for s in range(3):
        p = proj[:, s * width : (s + 1) * width]
        z = jnp.zeros_like(p)
        for i in range(TAPS):
            z = z + conv_ref[s, i : i + 1, :] * shifted(p, TAPS - 1 - i, wide_row)
        sigma = 1.0 / (1.0 + jnp.exp(-z))
        before.append(z)
        gate.append(sigma)
        active.append(z * sigma)

    scale = 1.0 / math.sqrt(HEAD)
    kept = []
    for h in range(heads):
        cut = slice(h * HEAD, (h + 1) * HEAD)
        aq, ak, v = active[0][:, cut], active[1][:, cut], active[2][:, cut]
        nq = lax.rsqrt(jnp.sum(aq * aq, 1, keepdims=True) + 1e-6)
        nk = lax.rsqrt(jnp.sum(ak * ak, 1, keepdims=True) + 1e-6)
        uq, k = aq * nq, ak * nk
        beta = strength[:, heads + h : heads + h + 1]
        held = head_forward(uq * scale, k, v, beta, cumulative[:, h : h + 1], cumulative_t[h : h + 1, :], within, strict, xor)
        out = held[-1]
        r = lax.rsqrt(jnp.mean(out * out, 1, keepdims=True) + 1e-5)
        normed = out * r
        core_low[:, cut] = (normed * gain).astype(BF16)
        kept.append((nq, nk, uq, k, v, beta, held[:-1], r, normed))

    part_half = part // 2
    ends = [slice(0, part_half), slice(part_half, part)]
    opposite = nx == 4
    ways = [1, -1] if opposite else [1]

    def along_x(a, sz, t, side, h):
        rows = pl.ds(h * part_half, part_half)
        return remote(
            parts.at[a, t, rows], r1.at[a, side, sz, rows], s1s.at[a, side, sz, h], s1r.at[a, side, sz, h], here.at_x(ways[side])
        )

    def across(a, sz, t, h):
        rows = pl.ds(h * part_half, part_half)
        return remote(parts.at[a, t, rows], relay.at[a, sz, h], s0s.at[a, sz, h], s0r.at[a, sz, h], here.at_x(ways[h]))

    def owner(sz, sx):
        return ((here.zh + sz) % nz) * nx + (here.x + sx + nx) % nx

    def pass_on(a, sz):
        for h, way in enumerate(ways if opposite else []):
            t = owner(sz, way)
            across(a, sz, t, h).wait_recv()
            parts[a, t, ends[h], :] = (parts[a, t, ends[h], :].astype(F32) + relay[a, sz, h].astype(F32)).astype(BF16)
            along_x(a, sz, t, h, h).start()

    def make(a, sz, build):
        zh = (here.zh + sz) % nz
        rows = pl.ds(pl.multiple_of(zh * nx * part, 16), nx * part)
        parts[a, pl.ds(zh * nx, nx)] = build(rows).astype(BF16).reshape(nx, part, LEN)
        if not isinstance(sz, int):
            ship(a, sz)

    def ship_across(a, sz):
        for h in range(2):
            across(a, sz, owner(sz, 2), h).start()

    def ship_along(a, sz, side):
        for h in range(2):
            if not opposite or h != side:
                along_x(a, sz, owner(sz, ways[side]), side, h).start()

    def ship(a, sz):
        if opposite:
            ship_across(a, sz)
        for side in range(len(ways)):
            ship_along(a, sz, side)

    away = [2, 1, 3] if nz == 4 else [1]

    def each_away(body):
        def step(i, _):
            body(jnp.where(i < 2, 2 - i, 3) if nz == 4 else i + 1)
            return 0

        lax.fori_loop(0, nz - 1, step, 0)

    def second(a, steps):
        for sz in steps:
            total = parts[a, owner(sz, 0)].astype(F32)
            for side in range(len(ways)):
                for h in range(2):
                    along_x(a, sz, 0, side, h).wait_recv()
                total = total + r1[a, side, sz].astype(F32)
            if sz:
                mine[a, sz] = total.astype(BF16)
                send(mine.at[a, sz], r2.at[a, sz], s2s.at[a, sz], s2r.at[a, sz], here.at_zh(sz))
            else:
                keep[a] = total

    def last(a):
        total = keep[a]
        for sz in range(1, nz):
            arrive(r2.at[a, sz], s2s.at[a, sz], s2r.at[a, sz])
            total = total + r2[a, sz].astype(F32)
        res_ref[a] = total.astype(BF16)

    def out_part(rows):
        return dot(wf[3, rows, :], core_low[...], NT)

    each_away(lambda sz: make(0, sz, out_part))

    def back_term(t, _):
        back[...] += dot(gr[t], wf[3, pl.ds(pl.multiple_of(t * part, 16), part), :])
        return 0

    lax.fori_loop(0, tensor, back_term, 0)
    make(0, 0, out_part)
    each_away(lambda sz: pass_on(0, sz))

    gain_grad = jnp.zeros((1, HEAD), F32)
    for h in range(heads):
        gain_grad = gain_grad + jnp.sum(back[:, h * HEAD : (h + 1) * HEAD] * kept[h][-1], 0, keepdims=True)
    gx[here.x] = jnp.concatenate([gain_grad, jnp.zeros((7, HEAD), F32)], 0)
    for s in range(1, nx):
        send(gx.at[here.x], gx.at[here.x], gxs.at[s - 1], gxr.at[s - 1], here.at_x(s))

    d_active = [[None] * heads for _ in range(3)]
    dc_all = jnp.zeros((LEN, LEN), F32)
    db_all = jnp.zeros((LEN, LEN), F32)
    for h in range(heads):
        nq, nk, uq, k, v, beta, held, r, normed = kept[h]
        dn = back[:, h * HEAD : (h + 1) * HEAD] * gain
        d_out = r * (dn - normed * jnp.mean(dn * normed, 1, keepdims=True))
        dq, dk, dv, dc, d_beta = head_backward(uq * scale, k, v, beta, *held, d_out, within, strict)
        dq = dq * scale
        d_active[0][h] = nq * (dq - uq * jnp.sum(uq * dq, 1, keepdims=True))
        d_active[1][h] = nk * (dk - k * jnp.sum(k * dk, 1, keepdims=True))
        d_active[2][h] = dv
        dc_all = jnp.where(lane == h, dc, dc_all)
        db_all = jnp.where(lane == heads + h, d_beta, db_all)

    for s in range(1, nx):
        arrive(gx.at[back_of(s, nx, here.x)], gxs.at[s - 1], gxr.at[s - 1])
    gz[here.zh] = sum(gx[i] for i in range(nx))
    for s in range(1, nz):
        send(gz.at[here.zh], gz.at[here.zh], gzs.at[s - 1], gzr.at[s - 1], here.at_zh(s))

    d_decay = triangle_product(triangle_t, dc_all)
    d_pre = -rate * d_decay / (1.0 + jnp.exp(-pre))
    pack[gate_tiles + 3, 1:2, :] = jnp.sum(-soft * d_decay, 0, keepdims=True)
    pack[gate_tiles + 3, 2:3, :] = jnp.sum(d_pre, 0, keepdims=True)
    d_logits = (d_pre + db_all * strength * (1.0 - strength)).astype(BF16)
    low[:, 3 * width :] = d_logits
    d_logits_t = d_logits.astype(F32).T[0:16, :].astype(BF16)

    for s in range(3):
        z, sigma = before[s], gate[s]
        dz = jnp.concatenate(d_active[s], 1) * (sigma * (1.0 + z * (1.0 - sigma)))
        p = proj[:, s * width : (s + 1) * width]
        dp_s = jnp.zeros_like(p)
        for i in range(TAPS):
            ahead = shifted(dz, i + 1 - TAPS, wide_row)
            dp_s = dp_s + conv_ref[s, i : i + 1, :] * ahead
            total = jnp.sum(ahead * p, 0, keepdims=True)
            for j in range(width // 128):
                at = j * TAPS + i
                pack[gate_tiles + s, at : at + 1, :] = total[:, j * 128 : (j + 1) * 128]
        low[:, s * width : (s + 1) * width] = dp_s.astype(BF16)

    def grad_in(rows):
        total = dot(gcol[rows, :], low[:, 3 * width :], NT)
        for s in range(3):
            total = total + dot(wf[s, rows, :], low[:, s * width : (s + 1) * width], NT)
        return total

    each_away(lambda sz: make(1, sz, grad_in))
    make(1, 0, grad_in)

    def gates(i, _):
        grad = dot(d_logits_t, xt[pl.ds(pl.multiple_of(i * 256, 256), 256), :], NT)
        pack[i, 0:4, :] = grad[0:4, 0:128]
        pack[i, 4:8, :] = grad[0:4, 128:256]
        return 0

    lax.fori_loop(0, gate_tiles, gates, 0)

    for s in range(1, nz):
        arrive(gz.at[back_of(s, nz, here.zh)], gzs.at[s - 1], gzr.at[s - 1])
    pack[gate_tiles + 3, 0:1, :] = sum(gz[i, 0:1, :] for i in range(nz))
    for s in range(1, ny):
        there = (here.y + s) % ny
        send(pack.at[pl.ds(there * each, each)], ry.at[here.y], rys.at[s - 1], ryr.at[s - 1], here.at_y(s))
    ry[here.y] = pack[pl.ds(here.y * each, each)]

    second(0, away)
    each_away(lambda sz: pass_on(1, sz))
    ship(1, 0)
    ship(0, 0)

    for s in range(1, ny):
        arrive(ry.at[back_of(s, ny, here.y)], rys.at[s - 1], ryr.at[s - 1])
    rz[q] = sum(ry[i] for i in range(ny))
    for r in range(1, 4):
        send(rz.at[q], rz.at[q], rzs.at[r - 1], rzr.at[r - 1], at_q(r))

    second(1, away)
    pass_on(1, 0)
    pass_on(0, 0)

    for r in range(1, 4):
        arrive(rz.at[q ^ r], rzs.at[r - 1], rzr.at[r - 1])
    fin[...] = sum(rz[i] for i in range(4))
    for s in range(1, ny):
        send(fin, all_sums.at[here.y], ays.at[s - 1], ayr.at[s - 1], here.at_y(s))
    all_sums[here.y] = fin[...]

    second(1, [0])
    second(0, [0])
    last(0)

    for s in range(1, ny):
        arrive(all_sums.at[back_of(s, ny, here.y)], ays.at[s - 1], ayr.at[s - 1])
    for i in range(ny):
        sum_ref[i * each : (i + 1) * each] = all_sums[i]

    last(1)

    def finished(sz, _):
        for a in range(2):
            for h in range(2):
                for side in range(len(ways)):
                    along_x(a, sz, 0, side, h).wait_send()
                if opposite:
                    across(a, sz, 0, h).wait_send()
        return 0

    lax.fori_loop(0, nz, finished, 0)
    early.finish()
    late.finish()
    for copy in sent:
        copy.wait_send()


def layer(dp, tensor, w, wo, x, g, wg, conv, rate, bias, gain):
    ny = dp // (ZL * CORES)
    nz = 4 if tensor == 16 else 2
    nx = tensor // nz
    part = x.shape[0]
    model, width = part * tensor, w.shape[2]
    tiles = pl.cdiv(model // 256 + 4, ny) * ny
    each = tiles // ny
    any_spec = pl.BlockSpec(memory_space=pl.ANY)
    vmem = pl.BlockSpec(memory_space=pltpu.VMEM)
    smem = pl.BlockSpec(memory_space=pltpu.SMEM)
    dma = pltpu.SemaphoreType.DMA
    sems = [dma((4,))]
    for dims in (
        (nz - 1, 2), (nx - 1, nz, 2), (2, nz, 2), (2, 2, nz, 2), (2, nz), (nx - 1,), (nz - 1,), (ny - 1,), (3,), (ny - 1,),
    ):
        sems += [dma(dims), dma(dims)]
    sems += stream_sems(ny, True) + stream_sems(ny, False)
    return pl.pallas_call(
        functools.partial(layer_kernel, dp, tensor),
        name="layer",
        out_shape=(jax.ShapeDtypeStruct((2, part, LEN), BF16), jax.ShapeDtypeStruct((tiles, 8, 128), F32)),
        in_specs=[any_spec] * 4 + [vmem] * 2 + [smem] * 2 + [vmem],
        out_specs=(vmem,) * 2,
        scratch_shapes=[
            pltpu.VMEM((4, model, width), BF16),
            pltpu.VMEM((model, LEN), BF16),
            pltpu.VMEM((model, LEN), BF16),
            pltpu.VMEM((tensor, LEN, part), BF16),
            pltpu.VMEM((tensor, LEN, part), BF16),
            pltpu.VMEM((16, model), BF16),
            pltpu.VMEM((model, 128), BF16),
            pltpu.VMEM((LEN, 3 * width), F32),
            pltpu.VMEM((LEN, width), F32),
            pltpu.VMEM((LEN, width), BF16),
            pltpu.VMEM((LEN, 3 * width + 128), BF16),
            pltpu.VMEM((tiles, 8, 128), F32),
            pltpu.VMEM((2, tensor, part, LEN), BF16),
            pltpu.VMEM((2, 2, nz, part, LEN), BF16),
            pltpu.VMEM((2, nz, 2, part // 2, LEN), BF16),
            pltpu.VMEM((2, part, LEN), F32),
            pltpu.VMEM((2, nz, part, LEN), BF16),
            pltpu.VMEM((nx, 8, 128), F32),
            pltpu.VMEM((nz, 8, 128), F32),
            pltpu.VMEM((2, nz, part, LEN), BF16),
            pltpu.VMEM((ny, each, 8, 128), F32),
            pltpu.VMEM((4, each, 8, 128), F32),
            pltpu.VMEM((each, 8, 128), F32),
            pltpu.VMEM((ny, each, 8, 128), F32),
        ]
        + sems,
        compiler_params=pltpu.CompilerParams(collective_id=0, has_side_effects=True, vmem_limit_bytes=56 * 2**20),
    )(w, wo, x, g, wg, conv, rate, bias, gain)


def split_kernel(res_ref, sum_ref, out_ref, gin_ref, gates_ref, conv_ref, rate_ref, bias_ref, gain_ref):
    out_ref[...] = res_ref[0]
    gin_ref[...] = res_ref[1]
    heads = gates_ref.shape[1]
    count = gates_ref.shape[2] // 256
    for i in range(count):
        for j in range(2):
            for s in range(2):
                at = j * 4 + s * heads
                gates_ref[s, :, i * 256 + j * 128 : i * 256 + (j + 1) * 128] = sum_ref[i, at : at + heads, :]
    for s in range(3):
        for j in range(2):
            conv_ref[s, :, j * 128 : (j + 1) * 128] = sum_ref[count + s, j * 4 : j * 4 + 4, :]
    rest = sum_ref[count + 3]
    row = lax.broadcasted_iota(jnp.int32, rest.shape, 0)
    lane = lax.broadcasted_iota(jnp.int32, rest.shape, 1)
    for h in range(heads):
        rate_ref[h] = jnp.sum(jnp.where((row == 1) & (lane == h), rest, 0.0))
        bias_ref[h] = jnp.sum(jnp.where((row == 2) & (lane == h), rest, 0.0))
    gain_ref[...] = rest[0:1, :]


def on_device(dp, tensor, inputs, w_qkv, w_gates, conv_weight, decay_rate, gate_bias, norm_gain, w_out, grad_out):
    part, model = inputs.shape[2], w_gates.shape[1]
    heads, width = decay_rate.shape[0], w_qkv.shape[2]
    res, total = layer(
        dp, tensor, w_qkv, w_out.T, inputs[0].T, grad_out[0].T, w_gates.transpose(0, 2, 1), conv_weight,
        decay_rate, gate_bias, norm_gain[None],
    )
    vmem = pl.BlockSpec(memory_space=pltpu.VMEM)
    smem = pl.BlockSpec(memory_space=pltpu.SMEM)
    out, grad_in, gates, conv, rate, bias, gain = pl.pallas_call(
        split_kernel,
        name="split",
        out_shape=(
            jax.ShapeDtypeStruct((part, LEN), BF16),
            jax.ShapeDtypeStruct((part, LEN), BF16),
            jax.ShapeDtypeStruct((2, heads, model), F32),
            jax.ShapeDtypeStruct((3, TAPS, width), F32),
            jax.ShapeDtypeStruct((heads,), F32),
            jax.ShapeDtypeStruct((heads,), F32),
            jax.ShapeDtypeStruct((1, HEAD), F32),
        ),
        in_specs=[vmem] * 2,
        out_specs=(vmem,) * 4 + (smem,) * 2 + (vmem,),
    )(res, total)
    return (out.T[None], grad_in.T[None], gates.transpose(0, 2, 1), conv, rate, bias, gain[0])


def solution(mesh):
    dp, tensor = mesh.shape["dp"], mesh.shape["tensor"]
    return jax.shard_map(
        functools.partial(on_device, dp, tensor),
        mesh=mesh,
        in_specs=(
            P("dp", None, "tensor"),
            P(None, "dp", "tensor"),
            P(None, None, "tensor"),
            P(None, None, "tensor"),
            P("tensor"),
            P("tensor"),
            P(),
            P("tensor", "dp"),
            P("dp", None, "tensor"),
        ),
        out_specs=(
            P("dp", None, "tensor"),
            P("dp", None, "tensor"),
            P(None, None, "tensor"),
            P(None, None, "tensor"),
            P("tensor"),
            P("tensor"),
            P(),
        ),
        check_vma=False,
    )
```

```python
import functools
import math

import jax
import jax.numpy as jnp
from jax import lax
from jax.experimental import pallas as pl
from jax.experimental.pallas import tpu as pltpu
from jax.sharding import PartitionSpec as P

MESH = pl.DeviceIdType.MESH
F32, BF16 = jnp.float32, jnp.bfloat16
LEN = 128
HEAD = 128
TAPS = 4
CORES = 2
ZL = 2
EARLY = 2
NN = (((1,), (0,)), ((), ()))
NT = (((1,), (1,)), ((), ()))


class Place:
    def __init__(self, dp, tensor):
        self.ny = dp // (ZL * CORES)
        self.nz = 4 if tensor == 16 else 2
        self.nx = tensor // self.nz
        d, t = lax.axis_index("dp"), lax.axis_index("tensor")
        self.d, self.t = d, t
        self.zl = d // (self.ny * CORES)
        self.y = (d // CORES) % self.ny
        self.c = d % CORES
        self.zh = t // self.nx
        self.x = t % self.nx

    def dp_of(self, zl, y, c):
        return zl * (self.ny * CORES) + y * CORES + c

    def at_y(self, step):
        return self.dp_of(self.zl, (self.y + step + self.ny) % self.ny, self.c), self.t

    def at_z(self):
        return self.dp_of(1 - self.zl, self.y, self.c), self.t

    def at_core(self):
        return self.dp_of(self.zl, self.y, 1 - self.c), self.t

    def at_zh(self, step):
        return self.d, ((self.zh + step + self.nz) % self.nz) * self.nx + self.x

    def at_x(self, step):
        return self.d, self.zh * self.nx + (self.x + step + self.nx) % self.nx


def remote(src, dst, send, recv, where):
    return pltpu.make_async_remote_copy(
        src_ref=src, dst_ref=dst, send_sem=send, recv_sem=recv, device_id=where, device_id_type=MESH
    )


def meet(peers):
    barrier = pltpu.get_barrier_semaphore()
    for where in peers:
        pl.semaphore_signal(barrier, inc=1, device_id=where, device_id_type=MESH)
    pl.semaphore_wait(barrier, len(peers))


def halves(a):
    high = a.astype(BF16)
    return high, (a - high.astype(F32)).astype(BF16)


def dot(a, b, dims=NN):
    return lax.dot_general(a, b, dims, preferred_element_type=F32)


def product(a, b, dims=NN):
    ah, al = halves(a)
    bh, bl = halves(b)
    side = 0 if dims is NN else 1
    return dot(jnp.concatenate([ah, ah, al], 1), jnp.concatenate([bh, bl, bh], side), dims)


def triangle_product(triangle, a):
    high = a.astype(BF16)
    rest = a - high.astype(F32)
    mid = rest.astype(BF16)
    low = (rest - mid.astype(F32)).astype(BF16)
    return dot(jnp.concatenate([triangle] * 3, 1), jnp.concatenate([high, mid, low], 0))


def unit_inverse(lower, xor):
    inverse = jnp.where(xor == 0, 1.0, 0.0) - jnp.where(xor == 1, lower, 0.0)
    width = 2
    while width < lower.shape[0]:
        between = jnp.where((xor >= width) & (xor < 2 * width), lower, 0.0)
        inverse = inverse - product(product(inverse, between), inverse)
        width *= 2
    return inverse


def head_forward(q, k, v, beta, c_col, c_row, within, strict, xor):
    fading = jnp.where(within, jnp.exp(jnp.where(within, c_col - c_row, 0.0)), 0.0)
    faded_keys = jnp.where(strict, fading * product(k, k, NT), 0.0)
    lower = beta * faded_keys
    inverse = unit_inverse(lower, xor)
    rows = product(inverse, beta * v)
    scores = fading * product(q, k, NT)
    return fading, faded_keys, lower, inverse, rows, scores, product(scores, rows)


def head_backward(q, k, v, beta, fading, faded_keys, lower, inverse, rows, scores, d_out, within, strict):
    d_scores = jnp.where(within, product(d_out, rows, NT), 0.0)
    d_rows = product(scores.T, d_out)
    d_target = product(inverse.T, d_rows)
    d_lower = jnp.where(strict, -product(d_target, rows, NT), 0.0)
    faded = fading * d_scores
    both = beta * fading * d_lower
    dq = product(faded, k)
    dk = product(faded.T, q) + product(both + both.T, k)
    dv = beta * d_target
    spread = d_scores * scores + d_lower * lower
    dc = jnp.sum(spread - spread.T, 1, keepdims=True)
    d_beta = jnp.sum(d_lower * faded_keys + d_target * v, 1, keepdims=True)
    return dq, dk, dv, dc, d_beta


def shifted(a, step, row):
    if step == 0:
        return a
    size = a.shape[0]
    moved = pltpu.roll(a, step % size, 0)
    keep = row >= step if step > 0 else row < size + step
    return jnp.where(keep, moved, 0.0)


class Stream:
    def __init__(self, here, early, full, shard, sems):
        self.here, self.early, self.full = here, early, full
        self.far = here.ny // 2
        self.shard, self.half = shard, shard // 2
        self.yp, self.ym, self.z, self.c = (sems[i : i + 2] for i in (0, 2, 4, 6))
        self.sent = []

    def block(self, p, place, h, other_core=False):
        here = self.here
        zl = here.zl if p == 0 else 1 - here.zl
        c = 1 - here.c if other_core else here.c
        d = here.dp_of(zl, (here.y - place + here.ny) % here.ny, c)
        return self.full.at[:, pl.ds(pl.multiple_of(d * self.shard + h * self.half, 16), self.half), :]

    def send(self, ref, sems, index, where):
        copy = remote(ref, ref, sems[0].at[index], sems[1].at[index], where)
        copy.start()
        self.sent.append(copy)

    def arrive(self, ref, sems, index):
        remote(ref, ref, sems[0].at[index], sems[1].at[index], self.here.at_core()).wait_recv()

    def travels(self, direction, k, h):
        return k < self.far or (k == self.far and h == (0 if direction > 0 else 1))

    def along_y(self, ref, direction, k, p, h):
        if self.travels(direction, k, h):
            self.send(ref, self.yp if direction > 0 else self.ym, (k - 1, p, h), self.here.at_y(direction))

    def along_z(self, ref, place, h):
        self.send(ref, self.z, (place, h), self.here.at_z())

    def to_core(self, ref, p, place, h):
        self.send(ref, self.c, (p, place, h), self.here.at_core())

    def start(self):
        for h in range(2):
            own = self.block(0, 0, h)
            self.along_y(own, 1, 1, 0, h)
            self.along_y(own, -1, 1, 0, h)

    def own_to_z(self):
        for h in range(2):
            self.along_z(self.block(0, 0, h), 0, h)

    def own_to_core(self):
        for h in range(2):
            self.to_core(self.block(0, 0, h), 0, 0, h)

    def places(self, k):
        return [k] if k in (0, self.far) else [k, self.here.ny - k]

    def from_z(self, k):
        if self.early and k:
            return
        for place in self.places(k):
            for h in range(2):
                got = self.block(1, place, h)
                self.arrive(got, self.z, (place, h))
                if self.early:
                    self.along_y(got, 1, 1, 1, h)
                    self.along_y(got, -1, 1, 1, h)
                self.to_core(got, 1, place, h)

    def from_y(self, k):
        for p in range(2 if self.early else 1):
            for h in range(2):
                for direction in (1, -1):
                    if not self.travels(direction, k, h):
                        continue
                    place = k if direction > 0 else self.here.ny - k
                    got = self.block(p, place, h)
                    self.arrive(got, self.yp if direction > 0 else self.ym, (k - 1, p, h))
                    self.along_y(got, direction, k + 1, p, h)
                    if not self.early:
                        self.along_z(got, place, h)
                    self.to_core(got, p, place, h)

    def from_core(self, k):
        for p in range(2):
            for place in self.places(k):
                for h in range(2):
                    self.arrive(self.block(p, place, h, True), self.c, (p, place, h))

    def finish(self):
        for copy in self.sent:
            copy.wait_send()


def stream_sems(ny, early):
    dma = pltpu.SemaphoreType.DMA
    sems = []
    for dims in ((ny // 2, 2 if early else 1, 2),) * 2 + ((1 if early else ny, 2), (2, ny, 2)):
        sems += [dma(dims), dma(dims)]
    return sems


def layer_kernel(
    dp, tensor, w_ref, wo_ref, x_ref, g_ref, wg_ref, conv_ref, rate_ref, bias_ref, gain_ref, res_ref, sum_ref, *scratch
):
    scratch = list(scratch)

    def take(n):
        out = scratch[:n]
        del scratch[:n]
        return out

    wf, xt, gt, xr, gr, wg16, gcol, proj, back, core_low, low, pack = take(12)
    parts, r1, relay, keep, r2, gx, gz, mine, ry, rz, fin, all_sums = take(12)
    own_sem, t1s, t1r, t2s, t2r, s0s, s0r, s1s, s1r, s2s, s2r, gxs, gxr, gzs, gzr, rys, ryr, rzs, rzr, ays, ayr = take(21)
    here = Place(dp, tensor)
    ny, nz, nx = here.ny, here.nz, here.nx
    far = ny // 2
    part = x_ref.shape[0]
    width = w_ref.shape[2]
    heads = width // HEAD
    each = pack.shape[0] // ny
    gate_tiles = xt.shape[0] // 256
    q = here.zl * CORES + here.c

    shard = w_ref.shape[1]
    early = Stream(here, True, wf.at[pl.ds(0, EARLY)], shard, take(8))
    late = Stream(here, False, wf.at[pl.ds(EARLY, 4 - EARLY)], shard, take(8))
    sent = []

    def at_q(r):
        other = q ^ r
        return here.dp_of(other // CORES, here.y, other % CORES), here.t

    def send(src, dst, s, r, where):
        copy = remote(src, dst, s, r, where)
        copy.start()
        sent.append(copy)

    def arrive(dst, s, r):
        remote(dst, dst, s, r, here.at_core()).wait_recv()

    def back_of(step, size, now):
        return (now - step + size) % size

    def slot(ref, t):
        return ref.at[pl.ds(pl.multiple_of(t * part, 16), part), :]

    mine_rows = pl.ds(pl.multiple_of(here.d * shard, 16), shard)
    own = [
        pltpu.make_async_copy(w_ref, wf.at[pl.ds(0, 3), mine_rows, :], own_sem.at[0]),
        pltpu.make_async_copy(wo_ref, wf.at[3, mine_rows, :], own_sem.at[1]),
        pltpu.make_async_copy(x_ref, slot(xt, here.t), own_sem.at[2]),
        pltpu.make_async_copy(g_ref, slot(gt, here.t), own_sem.at[3]),
    ]
    for copy in own:
        copy.start()
    meet(
        [here.at_y(s) for s in range(1, ny)]
        + [at_q(r) for r in range(1, 4)]
        + [here.at_zh(s) for s in range(1, nz)]
        + [here.at_x(s) for s in range(1, nx)]
    )

    arrays = (xt, gt)

    def set_out(a):
        got = slot(arrays[a], here.t)
        for s in sorted({1, nz - 1}):
            send(got, got, t1s.at[s - 1, a], t1r.at[s - 1, a], here.at_zh(s))
        for s in range(1, nx):
            send(got, got, t2s.at[s - 1, 0, a], t2r.at[s - 1, 0, a], here.at_x(s))

    for copy in own:
        copy.wait()
    early.own_to_z()
    late.start()
    early.start()
    set_out(0)
    late.own_to_z()
    late.own_to_core()
    early.own_to_core()
    early.from_z(0)

    proj[...] = jnp.zeros_like(proj)
    back[...] = jnp.zeros_like(back)
    pack[...] = jnp.zeros_like(pack)
    wide = wg_ref[...].astype(F32)
    wg16[...] = jnp.concatenate([wide[0], wide[1], jnp.zeros((16 - 2 * heads, wide.shape[2]), F32)], 0).astype(BF16)

    def column(i, _):
        at = pl.ds(pl.multiple_of(i * 128, 128), 128)
        tall = jnp.concatenate([wg16[:, at].astype(F32), jnp.zeros((112, 128), F32)], 0)
        gcol[at, :] = tall.T.astype(BF16)
        return 0

    lax.fori_loop(0, xt.shape[0] // 128, column, 0)

    row = lax.broadcasted_iota(jnp.int32, (LEN, LEN), 0)
    lane = lax.broadcasted_iota(jnp.int32, (LEN, LEN), 1)
    wide_row = lax.broadcasted_iota(jnp.int32, (LEN, width), 0)
    within, strict, xor = row >= lane, row > lane, row ^ lane
    triangle = jnp.where(within, 1.0, 0.0).astype(BF16)
    triangle_t = jnp.where(row <= lane, 1.0, 0.0).astype(BF16)
    lane_1 = lax.broadcasted_iota(jnp.int32, (1, LEN), 1)
    rate = sum(jnp.where(lane_1 == h, rate_ref[h], 0.0) for h in range(heads))
    bias = sum(jnp.where(lane_1 == h, bias_ref[h], 0.0) for h in range(heads))
    gain = gain_ref[...]

    def spread(a, steps):
        for s in steps:
            got = slot(arrays[a], back_of(s, nz, here.zh) * nx + here.x)
            arrive(got, t1s.at[s - 1, a], t1r.at[s - 1, a])
            if nz == 4 and s == (1 if a == 0 else 3):
                send(got, got, t1s.at[1, a], t1r.at[1, a], here.at_zh(1 if a == 0 else -1))
            for sx in range(1, nx):
                send(got, got, t2s.at[sx - 1, s, a], t2r.at[sx - 1, s, a], here.at_x(sx))

    near, further = sorted({1, nz - 1}), [2] if nz == 4 else []

    def landed(a, turned):
        dst = arrays[a]
        for s in range(nz):
            for sx in range(1, nx):
                got = slot(dst, back_of(s, nz, here.zh) * nx + back_of(sx, nx, here.x))
                arrive(got, t2s.at[sx - 1, s, a], t2r.at[sx - 1, s, a])

        def turn(t, _):
            turned[t] = dst[pl.ds(pl.multiple_of(t * part, 16), part), :].T
            return 0

        lax.fori_loop(0, tensor, turn, 0)

    def decays():
        logits_t = dot(wg16[...], xt[...])
        logits = jnp.concatenate([logits_t, jnp.zeros((LEN - 16, LEN), F32)], 0).T
        pre = logits + bias
        soft = jnp.maximum(pre, 0.0) + jnp.log1p(jnp.exp(-jnp.abs(pre)))
        strength = 1.0 / (1.0 + jnp.exp(-logits))
        cumulative = triangle_product(triangle, -rate * soft)
        cumulative_t = cumulative.T
        return logits, pre, soft, strength, cumulative, cumulative_t

    def contract(k):
        early.from_core(k)
        late.from_core(k)
        ways = len(early.places(k))

        def term(i, _):
            zl = jnp.where(i // ways == 0, here.zl, 1 - here.zl)
            step = jnp.where(i % ways == 0, k, ny - k)
            t = zl * ny + (here.y - step + ny) % ny
            rows = pl.ds(pl.multiple_of(t * part, 16), part)
            x = xr[t]
            for s in range(3):
                proj[:, s * width : (s + 1) * width] += dot(x, wf[s, rows, :])
            return 0

        lax.fori_loop(0, 2 * ways, term, 0)

    for k in range(1, far + 1):
        deep = k == far and far > 2
        if deep:
            landed(0, xr)
            for j in range(far - 1):
                contract(j)
        late.from_y(k)
        if deep:
            late.from_z(k - 1)
            landed(1, gr)
            contract(k - 1)
            logits, pre, soft, strength, cumulative, cumulative_t = decays()
        early.from_y(k)
        if not deep:
            late.from_z(k - 1)
        if k == 1:
            spread(0, near)
            set_out(1)
        if k == min(2, far):
            spread(0, further)
            spread(1, near)
        if k == min(3, far):
            spread(1, further)
    late.from_z(far)
    if far <= 2:
        landed(0, xr)
        landed(1, gr)
        logits, pre, soft, strength, cumulative, cumulative_t = decays()
        for j in range(far):
            contract(j)
    contract(far)

    before, gate, active = [], [], []
    for s in range(3):
        p = proj[:, s * width : (s + 1) * width]
        z = jnp.zeros_like(p)
        for i in range(TAPS):
            z = z + conv_ref[s, i : i + 1, :] * shifted(p, TAPS - 1 - i, wide_row)
        sigma = 1.0 / (1.0 + jnp.exp(-z))
        before.append(z)
        gate.append(sigma)
        active.append(z * sigma)

    scale = 1.0 / math.sqrt(HEAD)
    kept = []
    for h in range(heads):
        cut = slice(h * HEAD, (h + 1) * HEAD)
        aq, ak, v = active[0][:, cut], active[1][:, cut], active[2][:, cut]
        nq = lax.rsqrt(jnp.sum(aq * aq, 1, keepdims=True) + 1e-6)
        nk = lax.rsqrt(jnp.sum(ak * ak, 1, keepdims=True) + 1e-6)
        uq, k = aq * nq, ak * nk
        beta = strength[:, heads + h : heads + h + 1]
        held = head_forward(uq * scale, k, v, beta, cumulative[:, h : h + 1], cumulative_t[h : h + 1, :], within, strict, xor)
        out = held[-1]
        r = lax.rsqrt(jnp.mean(out * out, 1, keepdims=True) + 1e-5)
        normed = out * r
        core_low[:, cut] = (normed * gain).astype(BF16)
        kept.append((nq, nk, uq, k, v, beta, held[:-1], r, normed))

    part_half = part // 2
    ends = [slice(0, part_half), slice(part_half, part)]
    opposite = nx == 4
    ways = [1, -1] if opposite else [1]

    def along_x(a, sz, t, side, h):
        rows = pl.ds(h * part_half, part_half)
        return remote(
            parts.at[a, t, rows], r1.at[a, side, sz, rows], s1s.at[a, side, sz, h], s1r.at[a, side, sz, h], here.at_x(ways[side])
        )

    def across(a, sz, t, h):
        rows = pl.ds(h * part_half, part_half)
        return remote(parts.at[a, t, rows], relay.at[a, sz, h], s0s.at[a, sz, h], s0r.at[a, sz, h], here.at_x(ways[h]))

    def owner(sz, sx):
        return ((here.zh + sz) % nz) * nx + (here.x + sx + nx) % nx

    def pass_on(a, sz):
        for h, way in enumerate(ways if opposite else []):
            t = owner(sz, way)
            across(a, sz, t, h).wait_recv()
            parts[a, t, ends[h], :] = (parts[a, t, ends[h], :].astype(F32) + relay[a, sz, h].astype(F32)).astype(BF16)
            along_x(a, sz, t, h, h).start()

    def make(a, sz, build):
        zh = (here.zh + sz) % nz
        rows = pl.ds(pl.multiple_of(zh * nx * part, 16), nx * part)
        parts[a, pl.ds(zh * nx, nx)] = build(rows).astype(BF16).reshape(nx, part, LEN)
        if not isinstance(sz, int):
            ship(a, sz)

    def ship_across(a, sz):
        for h in range(2):
            across(a, sz, owner(sz, 2), h).start()

    def ship_along(a, sz, side):
        for h in range(2):
            if not opposite or h != side:
                along_x(a, sz, owner(sz, ways[side]), side, h).start()

    def ship(a, sz):
        if opposite:
            ship_across(a, sz)
        for side in range(len(ways)):
            ship_along(a, sz, side)

    away = [2, 1, 3] if nz == 4 else [1]

    def each_away(body):
        def step(i, _):
            body(jnp.where(i < 2, 2 - i, 3) if nz == 4 else i + 1)
            return 0

        lax.fori_loop(0, nz - 1, step, 0)

    def second(a, steps):
        for sz in steps:
            total = parts[a, owner(sz, 0)].astype(F32)
            for side in range(len(ways)):
                for h in range(2):
                    along_x(a, sz, 0, side, h).wait_recv()
                total = total + r1[a, side, sz].astype(F32)
            if sz:
                mine[a, sz] = total.astype(BF16)
                send(mine.at[a, sz], r2.at[a, sz], s2s.at[a, sz], s2r.at[a, sz], here.at_zh(sz))
            else:
                keep[a] = total

    def last(a):
        total = keep[a]
        for sz in range(1, nz):
            arrive(r2.at[a, sz], s2s.at[a, sz], s2r.at[a, sz])
            total = total + r2[a, sz].astype(F32)
        res_ref[a] = total.astype(BF16)

    def out_part(rows):
        return dot(wf[3, rows, :], core_low[...], NT)

    each_away(lambda sz: make(0, sz, out_part))

    def back_term(t, _):
        back[...] += dot(gr[t], wf[3, pl.ds(pl.multiple_of(t * part, 16), part), :])
        return 0

    lax.fori_loop(0, tensor, back_term, 0)

    gain_grad = jnp.zeros((1, HEAD), F32)
    for h in range(heads):
        gain_grad = gain_grad + jnp.sum(back[:, h * HEAD : (h + 1) * HEAD] * kept[h][-1], 0, keepdims=True)
    gx[here.x] = jnp.concatenate([gain_grad, jnp.zeros((7, HEAD), F32)], 0)
    for s in range(1, nx):
        send(gx.at[here.x], gx.at[here.x], gxs.at[s - 1], gxr.at[s - 1], here.at_x(s))

    d_active = [[None] * heads for _ in range(3)]
    dc_all = jnp.zeros((LEN, LEN), F32)
    db_all = jnp.zeros((LEN, LEN), F32)
    for h in range(heads):
        nq, nk, uq, k, v, beta, held, r, normed = kept[h]
        dn = back[:, h * HEAD : (h + 1) * HEAD] * gain
        d_out = r * (dn - normed * jnp.mean(dn * normed, 1, keepdims=True))
        dq, dk, dv, dc, d_beta = head_backward(uq * scale, k, v, beta, *held, d_out, within, strict)
        dq = dq * scale
        d_active[0][h] = nq * (dq - uq * jnp.sum(uq * dq, 1, keepdims=True))
        d_active[1][h] = nk * (dk - k * jnp.sum(k * dk, 1, keepdims=True))
        d_active[2][h] = dv
        dc_all = jnp.where(lane == h, dc, dc_all)
        db_all = jnp.where(lane == heads + h, d_beta, db_all)

    each_away(lambda sz: pass_on(0, sz))

    for s in range(1, nx):
        arrive(gx.at[back_of(s, nx, here.x)], gxs.at[s - 1], gxr.at[s - 1])
    gz[here.zh] = sum(gx[i] for i in range(nx))
    for s in range(1, nz):
        send(gz.at[here.zh], gz.at[here.zh], gzs.at[s - 1], gzr.at[s - 1], here.at_zh(s))

    d_decay = triangle_product(triangle_t, dc_all)
    d_pre = -rate * d_decay / (1.0 + jnp.exp(-pre))
    pack[gate_tiles + 3, 1:2, :] = jnp.sum(-soft * d_decay, 0, keepdims=True)
    pack[gate_tiles + 3, 2:3, :] = jnp.sum(d_pre, 0, keepdims=True)
    d_logits = (d_pre + db_all * strength * (1.0 - strength)).astype(BF16)
    low[:, 3 * width :] = d_logits
    d_logits_t = d_logits.astype(F32).T[0:16, :].astype(BF16)

    for s in range(3):
        z, sigma = before[s], gate[s]
        dz = jnp.concatenate(d_active[s], 1) * (sigma * (1.0 + z * (1.0 - sigma)))
        p = proj[:, s * width : (s + 1) * width]
        dp_s = jnp.zeros_like(p)
        for i in range(TAPS):
            ahead = shifted(dz, i + 1 - TAPS, wide_row)
            dp_s = dp_s + conv_ref[s, i : i + 1, :] * ahead
            total = jnp.sum(ahead * p, 0, keepdims=True)
            for j in range(width // 128):
                at = j * TAPS + i
                pack[gate_tiles + s, at : at + 1, :] = total[:, j * 128 : (j + 1) * 128]
        low[:, s * width : (s + 1) * width] = dp_s.astype(BF16)

    def grad_in(rows):
        total = dot(gcol[rows, :], low[:, 3 * width :], NT)
        for s in range(3):
            total = total + dot(wf[s, rows, :], low[:, s * width : (s + 1) * width], NT)
        return total

    each_away(lambda sz: make(1, sz, grad_in))
    make(1, 0, grad_in)
    make(0, 0, out_part)

    def gates(i, _):
        grad = dot(d_logits_t, xt[pl.ds(pl.multiple_of(i * 256, 256), 256), :], NT)
        pack[i, 0:4, :] = grad[0:4, 0:128]
        pack[i, 4:8, :] = grad[0:4, 128:256]
        return 0

    lax.fori_loop(0, gate_tiles, gates, 0)

    for s in range(1, nz):
        arrive(gz.at[back_of(s, nz, here.zh)], gzs.at[s - 1], gzr.at[s - 1])
    pack[gate_tiles + 3, 0:1, :] = sum(gz[i, 0:1, :] for i in range(nz))
    for s in range(1, ny):
        there = (here.y + s) % ny
        send(pack.at[pl.ds(there * each, each)], ry.at[here.y], rys.at[s - 1], ryr.at[s - 1], here.at_y(s))
    ry[here.y] = pack[pl.ds(here.y * each, each)]

    second(0, away)
    each_away(lambda sz: pass_on(1, sz))
    ship(1, 0)
    ship(0, 0)

    for s in range(1, ny):
        arrive(ry.at[back_of(s, ny, here.y)], rys.at[s - 1], ryr.at[s - 1])
    rz[q] = sum(ry[i] for i in range(ny))
    for r in range(1, 4):
        send(rz.at[q], rz.at[q], rzs.at[r - 1], rzr.at[r - 1], at_q(r))

    second(1, away)
    pass_on(1, 0)
    pass_on(0, 0)

    for r in range(1, 4):
        arrive(rz.at[q ^ r], rzs.at[r - 1], rzr.at[r - 1])
    fin[...] = sum(rz[i] for i in range(4))
    for s in range(1, ny):
        send(fin, all_sums.at[here.y], ays.at[s - 1], ayr.at[s - 1], here.at_y(s))
    all_sums[here.y] = fin[...]

    second(1, [0])
    second(0, [0])
    last(0)

    for s in range(1, ny):
        arrive(all_sums.at[back_of(s, ny, here.y)], ays.at[s - 1], ayr.at[s - 1])
    for i in range(ny):
        sum_ref[i * each : (i + 1) * each] = all_sums[i]

    last(1)

    def finished(sz, _):
        for a in range(2):
            for h in range(2):
                for side in range(len(ways)):
                    along_x(a, sz, 0, side, h).wait_send()
                if opposite:
                    across(a, sz, 0, h).wait_send()
        return 0

    lax.fori_loop(0, nz, finished, 0)
    early.finish()
    late.finish()
    for copy in sent:
        copy.wait_send()


def layer(dp, tensor, w, wo, x, g, wg, conv, rate, bias, gain):
    ny = dp // (ZL * CORES)
    nz = 4 if tensor == 16 else 2
    nx = tensor // nz
    part = x.shape[0]
    model, width = part * tensor, w.shape[2]
    tiles = pl.cdiv(model // 256 + 4, ny) * ny
    each = tiles // ny
    any_spec = pl.BlockSpec(memory_space=pl.ANY)
    vmem = pl.BlockSpec(memory_space=pltpu.VMEM)
    smem = pl.BlockSpec(memory_space=pltpu.SMEM)
    dma = pltpu.SemaphoreType.DMA
    sems = [dma((4,))]
    for dims in (
        (nz - 1, 2), (nx - 1, nz, 2), (2, nz, 2), (2, 2, nz, 2), (2, nz), (nx - 1,), (nz - 1,), (ny - 1,), (3,), (ny - 1,),
    ):
        sems += [dma(dims), dma(dims)]
    sems += stream_sems(ny, True) + stream_sems(ny, False)
    return pl.pallas_call(
        functools.partial(layer_kernel, dp, tensor),
        name="layer",
        out_shape=(jax.ShapeDtypeStruct((2, part, LEN), BF16), jax.ShapeDtypeStruct((tiles, 8, 128), F32)),
        in_specs=[any_spec] * 4 + [vmem] * 2 + [smem] * 2 + [vmem],
        out_specs=(vmem,) * 2,
        scratch_shapes=[
            pltpu.VMEM((4, model, width), BF16),
            pltpu.VMEM((model, LEN), BF16),
            pltpu.VMEM((model, LEN), BF16),
            pltpu.VMEM((tensor, LEN, part), BF16),
            pltpu.VMEM((tensor, LEN, part), BF16),
            pltpu.VMEM((16, model), BF16),
            pltpu.VMEM((model, 128), BF16),
            pltpu.VMEM((LEN, 3 * width), F32),
            pltpu.VMEM((LEN, width), F32),
            pltpu.VMEM((LEN, width), BF16),
            pltpu.VMEM((LEN, 3 * width + 128), BF16),
            pltpu.VMEM((tiles, 8, 128), F32),
            pltpu.VMEM((2, tensor, part, LEN), BF16),
            pltpu.VMEM((2, 2, nz, part, LEN), BF16),
            pltpu.VMEM((2, nz, 2, part // 2, LEN), BF16),
            pltpu.VMEM((2, part, LEN), F32),
            pltpu.VMEM((2, nz, part, LEN), BF16),
            pltpu.VMEM((nx, 8, 128), F32),
            pltpu.VMEM((nz, 8, 128), F32),
            pltpu.VMEM((2, nz, part, LEN), BF16),
            pltpu.VMEM((ny, each, 8, 128), F32),
            pltpu.VMEM((4, each, 8, 128), F32),
            pltpu.VMEM((each, 8, 128), F32),
            pltpu.VMEM((ny, each, 8, 128), F32),
        ]
        + sems,
        compiler_params=pltpu.CompilerParams(collective_id=0, has_side_effects=True, vmem_limit_bytes=56 * 2**20),
    )(w, wo, x, g, wg, conv, rate, bias, gain)


def split_kernel(res_ref, sum_ref, out_ref, gin_ref, gates_ref, conv_ref, rate_ref, bias_ref, gain_ref):
    out_ref[...] = res_ref[0]
    gin_ref[...] = res_ref[1]
    heads = gates_ref.shape[1]
    count = gates_ref.shape[2] // 256
    for i in range(count):
        for j in range(2):
            for s in range(2):
                at = j * 4 + s * heads
                gates_ref[s, :, i * 256 + j * 128 : i * 256 + (j + 1) * 128] = sum_ref[i, at : at + heads, :]
    for s in range(3):
        for j in range(2):
            conv_ref[s, :, j * 128 : (j + 1) * 128] = sum_ref[count + s, j * 4 : j * 4 + 4, :]
    rest = sum_ref[count + 3]
    row = lax.broadcasted_iota(jnp.int32, rest.shape, 0)
    lane = lax.broadcasted_iota(jnp.int32, rest.shape, 1)
    for h in range(heads):
        rate_ref[h] = jnp.sum(jnp.where((row == 1) & (lane == h), rest, 0.0))
        bias_ref[h] = jnp.sum(jnp.where((row == 2) & (lane == h), rest, 0.0))
    gain_ref[...] = rest[0:1, :]


def on_device(dp, tensor, inputs, w_qkv, w_gates, conv_weight, decay_rate, gate_bias, norm_gain, w_out, grad_out):
    part, model = inputs.shape[2], w_gates.shape[1]
    heads, width = decay_rate.shape[0], w_qkv.shape[2]
    res, total = layer(
        dp, tensor, w_qkv, w_out.T, inputs[0].T, grad_out[0].T, w_gates.transpose(0, 2, 1), conv_weight,
        decay_rate, gate_bias, norm_gain[None],
    )
    vmem = pl.BlockSpec(memory_space=pltpu.VMEM)
    smem = pl.BlockSpec(memory_space=pltpu.SMEM)
    out, grad_in, gates, conv, rate, bias, gain = pl.pallas_call(
        split_kernel,
        name="split",
        out_shape=(
            jax.ShapeDtypeStruct((part, LEN), BF16),
            jax.ShapeDtypeStruct((part, LEN), BF16),
            jax.ShapeDtypeStruct((2, heads, model), F32),
            jax.ShapeDtypeStruct((3, TAPS, width), F32),
            jax.ShapeDtypeStruct((heads,), F32),
            jax.ShapeDtypeStruct((heads,), F32),
            jax.ShapeDtypeStruct((1, HEAD), F32),
        ),
        in_specs=[vmem] * 2,
        out_specs=(vmem,) * 4 + (smem,) * 2 + (vmem,),
    )(res, total)
    return (out.T[None], grad_in.T[None], gates.transpose(0, 2, 1), conv, rate, bias, gain[0])


def solution(mesh):
    dp, tensor = mesh.shape["dp"], mesh.shape["tensor"]
    return jax.shard_map(
        functools.partial(on_device, dp, tensor),
        mesh=mesh,
        in_specs=(
            P("dp", None, "tensor"),
            P(None, "dp", "tensor"),
            P(None, None, "tensor"),
            P(None, None, "tensor"),
            P("tensor"),
            P("tensor"),
            P(),
            P("tensor", "dp"),
            P("dp", None, "tensor"),
        ),
        out_specs=(
            P("dp", None, "tensor"),
            P("dp", None, "tensor"),
            P(None, None, "tensor"),
            P(None, None, "tensor"),
            P("tensor"),
            P("tensor"),
            P(),
        ),
        check_vma=False,
    )
```
